128 devices in a mesh: tm: 64 (over y, z, x), space: 2 (over core).
Axes of the slice: x: 4, y: 4, z: 4, core: 2. Of those that a mesh axis runs over, the one named last changes fastest.
Arguments:
- states: float32 [512, 64, 512], P('tm', 'space'), may hold values from -6 to 6
- start: float32 [64, 512], P('space'), may hold values from -6 to 6
- control: float32 [512, 64, 512], P('tm', 'space'), may hold values from -6 to 6
- kappa: float32 [64, 512], P('space'), may hold values from 0.25 to 1.25
Outputs:
- updated: float32 [512, 64, 512], P('tm', 'space')
The draws below stay inside these ranges and needn't reach their ends.
All inputs are finite; a program needn't handle non-finite values.
Results may differ from the reference program's by a relative error of at most 0.00002.
Values sent between devices are 32-bit elements; how exact they have to be, the bound alone decides.
A program may use at most 128 MiB of HBM per device.

```python
import math
import jax
import jax.numpy as jnp
from jax import lax

GRID_COLS = 512
CHEB = 6
FACTOR = 4
STEPS = 512
GRID_ROWS = 64


def level_of(key, dims, shards, least, top_value):
    def one(dim, parts):
        heights = jax.random.uniform(jax.random.fold_in(jax.random.fold_in(key, 6), dim), (parts,), jnp.float32, least / len(shards), top_value / len(shards))
        return jnp.repeat(jnp.exp(heights), dims[dim] // parts).reshape((-1,) + (1,) * (len(dims) - dim - 1))

    factor_of = one(*shards[0])
    for cut in shards[1:]:
        factor_of = factor_of * one(*cut)
    return factor_of


def scatter_about(stream_key, dims, scale, reach, pieces=(), kind=jnp.bfloat16):
    result = scale * jax.random.normal(stream_key, dims, jnp.float32)
    if pieces:
        result = result * level_of(stream_key, dims, pieces, -0.22, 0.18)
    return jnp.clip(result, -reach, reach).astype(kind)


def setup_inputs(seed: int = 0) -> dict:
    seeds = jax.random.split(jax.random.key(seed), 5)
    return {
        "states": scatter_about(seeds[0], (STEPS, GRID_ROWS, GRID_COLS), 1.0, 6.0, ((0, 64), (1, 2)), jnp.float32),
        "start": scatter_about(seeds[1], (GRID_ROWS, GRID_COLS), 1.0, 6.0, ((0, 2),), jnp.float32),
        "control": scatter_about(seeds[2], (STEPS, GRID_ROWS, GRID_COLS), 1.0, 6.0, ((0, 64), (1, 2)), jnp.float32),
        "kappa": jnp.clip(jnp.exp(math.log(1.25) - 1.609438 * jax.random.uniform(seeds[3], (GRID_ROWS, GRID_COLS), jnp.float32) ** level_of(seeds[3], (GRID_ROWS, GRID_COLS), ((0, 2),), -0.2, 0.2)), 0.25, 1.25),
    }


step_size = 0.1
kappa_top = 1.25


def cheb_weights(step_scale):
    lowest = 1.0
    highest = 1.0 + 8.0 * step_scale * kappa_top
    centre_value = 0.5 * (highest + lowest)
    half_width = 0.5 * (highest - lowest)
    spread_ratio = centre_value / half_width
    rho_prev = 1.0 / spread_ratio
    weights = [(0.0, 1.0 / centre_value)]
    for sweep in range(1, CHEB):
        rho_next = 1.0 / (2.0 * spread_ratio - rho_prev)
        weights.append((rho_next * rho_prev, 2.0 * rho_next / half_width))
        rho_prev = rho_next
    return weights


def face_terms(kappa_rows):
    vertical = 0.5 * (kappa_rows[:-1] + kappa_rows[1:])
    sideways = jnp.pad(kappa_rows[1:-1], ((0, 0), (1, 1)))
    horizontal = 0.5 * (sideways[:, :-1] + sideways[:, 1:])
    face_up = vertical[:-1]
    face_down = vertical[1:]
    face_left = horizontal[:, :-1]
    face_right = horizontal[:, 1:]
    centre = ((face_up + face_down) + face_left) + face_right
    return face_up, face_down, face_left, face_right, centre


def apply_op(widened, face_set, step_scale):
    face_up, face_down, face_left, face_right, centre = face_set
    middle = widened[..., 1:-1, :]
    sideways = jnp.pad(middle, [(0, 0)] * (middle.ndim - 1) + [(1, 1)])
    neighbours = face_up * widened[..., :-2, :] + face_down * widened[..., 2:, :]
    neighbours = neighbours + face_left * sideways[..., :-2] + face_right * sideways[..., 2:]
    return middle + step_scale * (centre * middle - neighbours)


def pad_rows(field_now):
    return jnp.pad(field_now, [(0, 0)] * (field_now.ndim - 2) + [(1, 1), (0, 0)])


def advance(field_now, target, face_set, step_scale):
    iterate = field_now
    update = jnp.zeros_like(field_now)
    for keep_weight, new_weight in cheb_weights(step_scale):
        residue = target - apply_op(pad_rows(iterate), face_set, step_scale)
        update = keep_weight * update + new_weight * residue
        iterate = iterate + update
    return iterate


def reference(states, start, control, kappa):
    face_set = face_terms(jnp.pad(kappa, ((1, 1), (0, 0))))
    step_count = states.shape[0]
    intervals = step_count // FACTOR
    groups = states.reshape(intervals, FACTOR, GRID_ROWS, GRID_COLS)
    pushes = control.reshape(intervals, FACTOR, GRID_ROWS, GRID_COLS)

    def fine(field_now, source):
        return advance(field_now, field_now + step_size * source, face_set, step_size)

    def relax_points(groups):
        roots = jnp.concatenate([start[None], groups[:-1, FACTOR - 1]], 0)
        current = roots
        outputs = []
        for position in range(FACTOR - 1):
            current = fine(current, pushes[:, position])
            outputs.append(current)
        return jnp.concatenate([jnp.stack(outputs, 1), groups[:, FACTOR - 1:]], 1)

    groups = relax_points(groups)
    anchors = fine(groups[:, FACTOR - 2], pushes[:, FACTOR - 1])
    groups = jnp.concatenate([groups[:, :FACTOR - 1], anchors[:, None]], 1)
    groups = relax_points(groups)
    residue = fine(groups[:, FACTOR - 2], pushes[:, FACTOR - 1]) - groups[:, FACTOR - 1]
    coarse_scale = FACTOR * step_size

    def coarse_turn(error_now, piece):
        error_next = advance(error_now, error_now, face_set, coarse_scale) + piece
        return error_next, error_next

    unused, errors = lax.scan(coarse_turn, jnp.zeros((GRID_ROWS, GRID_COLS), jnp.float32), residue)
    corrected = groups[:, FACTOR - 1] + errors
    groups = jnp.concatenate([groups[:, :FACTOR - 1], corrected[:, None]], 1)
    return groups.reshape(step_count, GRID_ROWS, GRID_COLS)
```

```python
import functools

import jax
import jax.numpy as jnp
import numpy as np
from jax import lax
from jax.experimental import pallas as pl
from jax.experimental.pallas import tpu as pltpu
from jax.sharding import PartitionSpec as P

MESH = pl.DeviceIdType.MESH
CHEB = 6
FACTOR = 4
step_size = 0.1
kappa_top = 1.25
ROWS = 64
COLS = 512
HALF = ROWS // 2
WINDOW = 8
GRID = (8, 4, 8, 128)


def cheb_weights(step_scale):
    highest = 1.0 + 8.0 * step_scale * kappa_top
    centre_value = 0.5 * (highest + 1.0)
    half_width = 0.5 * (highest - 1.0)
    spread_ratio = centre_value / half_width
    rho_prev = 1.0 / spread_ratio
    weights = [(0.0, 1.0 / centre_value)]
    for _ in range(1, CHEB):
        rho_next = 1.0 / (2.0 * spread_ratio - rho_prev)
        weights.append((rho_next * rho_prev, 2.0 * rho_next / half_width))
        rho_prev = rho_next
    return weights


def factors(s):
    poly = np.polynomial.Polynomial
    x, d, one, m = poly([0.0]), poly([0.0]), poly([1.0]), poly([0.0, 1.0])
    for keep, new in cheb_weights(s):
        d = keep * d + new * (one - m * x)
        x = x + d
    lead = x.coef[5]
    roots = x.roots()
    real = [r.real for r in roots if abs(r.imag) < 1e-9]
    pairs = sorted((r.real, r.imag) for r in roots if r.imag > 1e-9)
    assert lead < 0 and len(real) == 1 and len(pairs) == 2
    kap = (-lead * s**6) ** (1.0 / 6.0)
    shifts = [0.0, kap * (1.0 - real[0]) / s] + [kap * (1.0 - p[0]) / s for p in pairs]
    betas = [(kap * p[1] / s) ** 2 for p in pairs]
    return float(kap), [float(v) for v in shifts], [float(v) for v in betas]


def sroll(x, by):
    return pltpu.roll(x, by % 8, 0)


def lroll(x, by):
    return pltpu.roll(x, by % 128, 1)


def put(buf, i, v, val):
    buf[i, v + 2] = val
    if v >= 2:
        buf[i, v - 2] = lroll(val, 1)
    else:
        buf[i, v + 6] = lroll(val, -1)


def pair(src, fx, fy, d_one, d_two, beta, source, emit):
    held, mid = {}, {}

    def y(i, c):
        if (i, c) not in held:
            if i == -1:
                held[i, c] = sroll(y(7, c), 1)
            elif i == 8:
                held[i, c] = sroll(y(0, c), -1)
            else:
                held[i, c] = src[i, c + 2]
        return held[i, c]

    def w(i, c):
        if (i, c) not in mid:
            mid[i, c] = sroll(mid[7, c], 1) if i == -1 else sroll(mid[0, c], -1)
        return mid[i, c]

    def apply(f, d, i, c):
        k = c + 1
        up_down = (d[i, k] * f(i, c) + fy[i, k] * f(i - 1, c)) + fy[i + 1, k] * f(i + 1, c)
        return up_down + (fx[i, k] * f(i, c - 1) + fx[i, k + 1] * f(i, c + 1))

    first, second = set(), set()
    for i in range(8):
        for c in range(-1, 5):
            val = apply(y, d_one, i, c)
            if source is not None:
                val = val + source(i, c)
            mid[i, c] = val
        first.add(i)
        for j in range(8):
            if j not in second and {(j - 1) % 8, j, (j + 1) % 8} <= first:
                for v in (0, 3, 1, 2):
                    val = apply(w, d_two, j, v)
                    if beta is not None:
                        val = val + beta * src[j, v + 2]
                    emit(j, v, val)
                second.add(j)


def solve(buf, tmp, coefs, betas, source, emit):
    fx, fy, d = coefs
    pair(buf, fx, fy, d.at[0], d.at[1], None, source, functools.partial(put, tmp.at[0]))
    pair(tmp.at[0], fx, fy, d.at[2], d.at[2], betas[0], None, functools.partial(put, tmp.at[1]))
    pair(tmp.at[1], fx, fy, d.at[3], d.at[3], betas[1], None, emit)


def move_columns(x, table):
    high = x.astype(jnp.bfloat16)
    rest = x - high.astype(jnp.float32)
    middle = rest.astype(jnp.bfloat16)
    low = (rest - middle.astype(jnp.float32)).astype(jnp.bfloat16)
    stacked = jnp.concatenate([high, middle, low], 0)
    out = jnp.dot(stacked, table, preferred_element_type=jnp.float32)
    n = x.shape[0]
    return (out[:n] + out[n : 2 * n]) + out[2 * n :]


def kernel(
    n_t, fine_set, coarse_set,
    states, start, control, kappa, out,
    nat, xp, table_in, table_out, kp, fx0, fy0, c0, fxf, fyf, df, fxc, fyc, dc,
    g, ub, tmp, old, wd, rb, nb, lb, dp, eb, lbuf, nat_f, nat_c,
    ss, rs, lrecv, esend, credit,
):
    t = lax.axis_index("tm")
    c = lax.axis_index("space")
    last = n_t - 1
    central = jnp.logical_and(t == last, c == 0)
    partner = (t, 1 - c)
    right = (t + 1, 0 * c)
    hub = (0 * t + last, 0 * c)
    mine = pl.multiple_of(c * HALF, HALF)
    theirs = pl.multiple_of((1 - c) * HALF, HALF)

    def remote(src, dst, k, dev):
        return pltpu.make_async_remote_copy(
            src_ref=src, dst_ref=dst, send_sem=ss.at[k], recv_sem=rs.at[k], device_id=dev, device_id_type=MESH
        )

    barrier = pltpu.get_barrier_semaphore()
    pl.semaphore_signal(barrier, inc=1, device_id=partner, device_id_type=MESH)

    @pl.when(jnp.logical_and(c == 0, t > 0))
    def _():
        pl.semaphore_signal(barrier, inc=1, device_id=(t - 1, 0 * c), device_id_type=MESH)
        pl.semaphore_signal(barrier, inc=1, device_id=(t - 1, 0 * c + 1), device_id_type=MESH)

    @pl.when(jnp.logical_and(c == 0, t < last))
    def _():
        pl.semaphore_signal(barrier, inc=1, device_id=hub, device_id_type=MESH)

    nat[0:4, pl.ds(mine, HALF), :] = control[pl.ds(4 * c, 4)]
    nat[6, pl.ds(mine, HALF), :] = kappa[...]

    @pl.when(c == 0)
    def _():
        nat[5, pl.ds(mine, HALF), :] = states[3]

        @pl.when(t == 0)
        def _():
            nat[4, pl.ds(mine, HALF), :] = start[...]

    @pl.when(c == 1)
    def _():
        nat[4, pl.ds(mine, HALF), :] = states[3]
        nat[5, pl.ds(mine, HALF), :] = states[7]

    down = lax.broadcasted_iota(jnp.int32, (COLS, COLS), 0)
    across = lax.broadcasted_iota(jnp.int32, (COLS, COLS), 1)
    table_in[...] = jnp.where(down == 4 * (across % 128) + across // 128, 1.0, 0.0).astype(jnp.bfloat16)
    table_out[...] = jnp.where(across == 4 * (down % 128) + down // 128, 1.0, 0.0).astype(jnp.bfloat16)

    pl.semaphore_wait(barrier, 1 + jnp.where(t < last, 1, 0) + jnp.where(central, last, 0))

    to_control = remote(control.at[pl.ds(4 * (1 - c), 4)], nat.at[pl.ds(0, 4), pl.ds(mine, HALF), :], 0, partner)
    to_kappa = remote(kappa, nat.at[6, pl.ds(mine, HALF), :], 3, partner)
    to_root = remote(states.at[3], nat.at[4, pl.ds(mine, HALF), :], 1, partner)
    to_next = remote(states.at[7], nat.at[5, pl.ds(mine, HALF), :], 2, partner)
    to_first = remote(states.at[3], nat.at[5, pl.ds(mine, HALF), :], 2, partner)
    to_start = remote(start, nat.at[4, pl.ds(mine, HALF), :], 1, partner)
    to_right = [remote(states.at[7], nat.at[4, pl.ds(k * HALF, HALF), :], 5 + k, right) for k in range(2)]

    for k in range(2):

        @pl.when(jnp.logical_and(t < last, c == k))
        def _():
            to_right[k].start()

    to_kappa.start()

    @pl.when(c == 0)
    def _():
        to_root.start()
        to_next.start()

    @pl.when(c == 1)
    def _():
        to_first.start()

        @pl.when(t == 0)
        def _():
            to_start.start()

    to_control.start()

    @pl.when(central)
    def _():
        def give(k, carry):
            pl.semaphore_signal(credit, inc=1, device_id=(k, 0 * c), device_id_type=MESH)
            return carry

        lax.fori_loop(0, min(WINDOW + 1, last), give, 0)

    def to_layout(x, use):
        moved = move_columns(x, table_in[...])
        for v in range(4):
            xp[v] = moved[:, 128 * v : 128 * (v + 1)]
        for i in range(8):
            for v in range(4):
                use(i, v, xp[v, pl.ds(i, 8, stride=8), :])

    def from_layout(give):
        for i in range(8):
            for v in range(4):
                xp[v, pl.ds(i, 8, stride=8), :] = give(i, v)
        return move_columns(jnp.concatenate([xp[v] for v in range(4)], 1), table_out[...])

    to_kappa.wait()

    def hold_kappa(i, v, val):
        kp[i, v] = val

    to_layout(nat[6], hold_kappa)
    lane = lax.broadcasted_iota(jnp.int32, (8, 128), 1)
    sub = lax.broadcasted_iota(jnp.int32, (8, 128), 0)
    zero = jnp.zeros((8, 128), jnp.float32)
    for i in range(8):
        row = [kp[i, v] for v in range(4)]
        after = jnp.where(lane < 127, lroll(row[0], -1), zero)
        before = jnp.where(lane > 0, lroll(row[3], 1), zero)
        wide = [before] + row + [after]
        side = [0.5 * (wide[k] + wide[k + 1]) for k in range(5)]
        inner_right = jnp.where(lane < 127, side[4], zero)
        inner = [jnp.where(lane > 0, side[0], zero), side[1], side[2], side[3], inner_right]
        for k in range(5):
            fx0[i, k + 1] = inner[k]
        fx0[i, 0] = lroll(side[3], 1)
        fx0[i, 6] = lroll(side[1], -1)
        for v in range(4):
            if i == 0:
                above = jnp.where(sub > 0, sroll(kp[7, v], 1), zero)
            else:
                above = kp[i - 1, v]
            if i == 7:
                below = jnp.where(sub < 7, sroll(kp[0, v], -1), zero)
            else:
                below = kp[i + 1, v]
            up = 0.5 * (above + row[v])
            low = 0.5 * (row[v] + below)
            centre = ((up + low) + side[v]) + side[v + 1]
            pieces = [(c0, i, centre), (fy0, i, jnp.where(sub > 0, up, zero) if i == 0 else up)]
            if i == 7:
                pieces.append((fy0, 8, jnp.where(sub < 7, low, zero)))
            for ref, at, val in pieces:
                ref[at, v + 1] = val
                if v == 3:
                    ref[at, 0] = lroll(val, 1)
                if v == 0:
                    ref[at, 5] = lroll(val, -1)

    def fill(kap, shifts, fx, fy, d):
        fx[...] = fx0[...] * (-kap)
        fy[...] = fy0[...] * (-kap)
        for k in range(4):
            d[k] = c0[...] * kap + shifts[k]

    fill(fine_set[0], fine_set[1], fxf, fyf, df)

    @pl.when(c == 0)
    def _():
        to_first.wait_recv()

        @pl.when(t == 0)
        def _():
            to_start.wait_recv()

        @pl.when(t > 0)
        def _():
            to_right[0].wait_recv()
            to_right[1].wait_recv()

    @pl.when(c == 1)
    def _():
        to_root.wait_recv()
        to_next.wait_recv()

    to_layout(nat[4], functools.partial(put, ub))

    def hold_old(i, v, val):
        old[i, v] = val

    to_layout(nat[5], hold_old)
    to_control.wait()

    def bring(j, carry):
        def hold(i, v, val):
            val = val * (-fine_set[0])
            g[j, i, v + 1] = val
            if v == 3:
                g[j, i, 0] = lroll(val, 1)
            if v == 0:
                g[j, i, 5] = lroll(val, -1)

        to_layout(nat[j], hold)
        return carry

    lax.fori_loop(0, 4, bring, 0)
    g[4] = jnp.zeros(g.shape[1:], jnp.float32)

    def fine(j, carry):
        @pl.when(j == 4)
        def _():
            for i in range(8):
                for v in range(4):
                    put(ub, i, v, wd[3, i, v] - old[i, v])

        source = g.at[jnp.minimum(j, 4)]

        def emit(i, v, val):
            val = val + ub[i, v + 2]
            put(ub, i, v, val)
            wd[j, i, v] = val

        solve(ub, tmp, (fxf, fyf, df), fine_set[2], lambda i, k: source[i, k + 1], emit)
        return carry

    lax.fori_loop(0, 8, fine, 0)

    to_r = remote(wd.at[7], rb, 7, partner)
    to_c = remote(wd.at[3], nb, 8, partner)
    to_d_partner = remote(wd.at[pl.ds(4, 3)], dp, 9, partner)
    to_d_right = remote(wd.at[pl.ds(4, 3)], dp, 9, right)
    to_hub = pltpu.make_async_remote_copy(
        src_ref=lb, dst_ref=lbuf.at[t], send_sem=ss.at[13], recv_sem=lrecv.at[t], device_id=hub, device_id_type=MESH
    )

    @pl.when(c == 1)
    def _():
        @pl.when(t < last)
        def _():
            to_r.start()
            to_d_right.start()

        to_c.start()

    fill(coarse_set[0], coarse_set[1], fxc, fyc, dc)
    coarse = (fxc, fyc, dc)

    def coarse_solve(emit):
        solve(ub, tmp, coarse, coarse_set[2], None, emit)

    @pl.when(c == 0)
    def _():
        to_d_partner.start()

        @pl.when(t < last)
        def _():
            def emit(i, v, val):
                lb[i, v] = val + ub[i, v + 2]

            coarse_solve(emit)
            to_r.wait_recv()
            lb[...] = lb[...] + rb[...]
            pl.semaphore_wait(credit, 1)
            to_hub.start()

    to_out_f = remote(
        nat_f.at[:, pl.ds(theirs, HALF), :], out.at[pl.ds(4 * c, 3)], 10, partner
    )

    def f_points():
        has = jnp.logical_or(c == 1, t > 0)

        @pl.when(has)
        def _():
            to_d_partner.wait_recv()

        @pl.when(jnp.logical_not(has))
        def _():
            dp[...] = jnp.zeros(dp.shape, jnp.float32)

        def one(j, carry):
            nat_f[j] = from_layout(lambda i, v: wd[j, i, v] + dp[j, i, v])
            return carry

        lax.fori_loop(0, 3, one, 0)
        to_out_f.start()
        out[pl.ds(4 * c, 3)] = nat_f[:, pl.ds(mine, HALF), :]

    @pl.when(jnp.logical_not(central))
    def _():
        f_points()

    def to_owner(k):
        return pltpu.make_async_remote_copy(
            src_ref=lbuf.at[k], dst_ref=eb, send_sem=esend.at[k], recv_sem=rs.at[14],
            device_id=(k + 1, 0 * c), device_id_type=MESH,
        )

    def landed(k):
        return pltpu.make_async_remote_copy(
            src_ref=lb, dst_ref=lbuf.at[k], send_sem=ss.at[13], recv_sem=lrecv.at[k], device_id=hub, device_id_type=MESH
        )

    @pl.when(central)
    def _():
        landed(0).wait_recv()
        to_owner(0).start()
        for i in range(8):
            for v in range(4):
                put(ub, i, v, lbuf[0, i, v])

        def turn(k, carry):
            @pl.when(k + WINDOW < last)
            def _():
                pl.semaphore_signal(credit, inc=1, device_id=(k + WINDOW, 0 * c), device_id_type=MESH)

            @pl.when(k == min(10, last - 1))
            def _():
                f_points()

            def emit_one(i, v, val):
                put(ub, i, v, val + ub[i, v + 2])

            coarse_solve(emit_one)
            landed(k).wait_recv()

            def emit_two(i, v, val):
                val = val + (ub[i, v + 2] + lbuf[k, i, v])
                put(ub, i, v, val)
                lbuf[k, i, v] = val

            coarse_solve(emit_two)

            @pl.when(k < last - 1)
            def _():
                to_owner(k).start()

            @pl.when(k >= 8)
            def _():
                to_owner(k - 8).wait_send()

            return carry

        lax.fori_loop(1, last, turn, 0)
        eb[...] = lbuf[last - 1]

    to_out_c = [
        remote(nat_c.at[k, pl.ds(HALF, HALF), :], out.at[4 * k + 3], 11 + k, partner) for k in range(2)
    ]

    @pl.when(c == 0)
    def _():
        to_c.wait_recv()

        @pl.when(t == 0)
        def _():
            eb[...] = jnp.zeros(eb.shape, jnp.float32)

        @pl.when(jnp.logical_and(t > 0, t < last))
        def _():
            to_owner(0).wait_recv()

        @pl.when(t < last)
        def _():
            for i in range(8):
                for v in range(4):
                    put(ub, i, v, eb[i, v])

        nat_c[0] = from_layout(lambda i, v: wd[3, i, v] + eb[i, v])
        to_out_c[0].start()

        def emit(i, v, val):
            eb[i, v] = (val + ub[i, v + 2]) + wd[7, i, v]

        coarse_solve(emit)
        nat_c[1] = from_layout(lambda i, v: nb[i, v] + eb[i, v])
        to_out_c[1].start()
        for k in range(2):
            out[4 * k + 3] = nat_c[k, 0:HALF, :]

    @pl.when(c == 1)
    def _():
        to_out_c[0].wait_recv()
        to_out_c[1].wait_recv()
        to_c.wait_send()
        to_first.wait_send()

        @pl.when(t == 0)
        def _():
            to_start.wait_send()

        @pl.when(t < last)
        def _():
            to_r.wait_send()
            to_d_right.wait_send()

    to_out_f.wait()
    for k in range(2):

        @pl.when(jnp.logical_and(t < last, c == k))
        def _():
            to_right[k].wait_send()

    @pl.when(c == 0)
    def _():
        to_out_c[0].wait_send()
        to_out_c[1].wait_send()
        to_root.wait_send()
        to_next.wait_send()
        to_d_partner.wait_send()

        @pl.when(t < last)
        def _():
            to_hub.wait_send()

    @pl.when(central)
    def _():
        def drain(k, carry):
            to_owner(k).wait_send()
            return carry

        lax.fori_loop(max(0, last - 8), last - 1, drain, 0)


def solution(mesh):
    n_t = mesh.shape["tm"]
    fine_set = factors(step_size)
    coarse_set = factors(FACTOR * step_size)
    f32 = jnp.float32

    def vmem(*shape):
        return pltpu.VMEM(shape, f32)

    def on_device(states, start, control, kappa):
        whole = pl.BlockSpec(memory_space=pltpu.VMEM)
        tile = (8, 128)
        return pl.pallas_call(
            functools.partial(kernel, n_t, fine_set, coarse_set),
            out_shape=jax.ShapeDtypeStruct((8, HALF, COLS), f32),
            in_specs=[whole] * 4,
            out_specs=whole,
            scratch_shapes=[
                vmem(7, ROWS, COLS),
                vmem(4, ROWS, 128),
                pltpu.VMEM((COLS, COLS), jnp.bfloat16),
                pltpu.VMEM((COLS, COLS), jnp.bfloat16),
                vmem(*GRID),
                vmem(8, 7, *tile), vmem(9, 6, *tile), vmem(8, 6, *tile),
                vmem(8, 7, *tile), vmem(9, 6, *tile), vmem(4, 8, 6, *tile),
                vmem(8, 7, *tile), vmem(9, 6, *tile), vmem(4, 8, 6, *tile),
                vmem(5, 8, 6, *tile),
                vmem(8, 8, *tile),
                vmem(2, 8, 8, *tile),
                vmem(*GRID),
                vmem(8, *GRID),
                vmem(*GRID), vmem(*GRID), vmem(*GRID),
                vmem(3, *GRID),
                vmem(*GRID),
                vmem(n_t - 1, *GRID),
                vmem(3, ROWS, COLS),
                vmem(2, ROWS, COLS),
                pltpu.SemaphoreType.DMA((15,)),
                pltpu.SemaphoreType.DMA((15,)),
                pltpu.SemaphoreType.DMA((n_t,)),
                pltpu.SemaphoreType.DMA((n_t,)),
                pltpu.SemaphoreType.REGULAR,
            ],
            compiler_params=pltpu.CompilerParams(
                collective_id=0, has_side_effects=True, vmem_limit_bytes=48 * 2**20
            ),
        )(states, start, control, kappa)

    return jax.shard_map(
        on_device,
        mesh=mesh,
        in_specs=(P("tm", "space", None), P("space", None), P("tm", "space", None), P("space", None)),
        out_specs=P("tm", "space", None),
        check_vma=False,
    )
```

```python
import functools

import jax
import jax.numpy as jnp
import numpy as np
from jax import lax
from jax.experimental import pallas as pl
from jax.experimental.pallas import tpu as pltpu
from jax.sharding import PartitionSpec as P

MESH = pl.DeviceIdType.MESH
CHEB = 6
FACTOR = 4
step_size = 0.1
kappa_top = 1.25
ROWS = 64
COLS = 512
HALF = ROWS // 2
WINDOW = 5
DIRECT = 4
GRID = (8, 4, 8, 128)


def cheb_weights(step_scale):
    highest = 1.0 + 8.0 * step_scale * kappa_top
    centre_value = 0.5 * (highest + 1.0)
    half_width = 0.5 * (highest - 1.0)
    spread_ratio = centre_value / half_width
    rho_prev = 1.0 / spread_ratio
    weights = [(0.0, 1.0 / centre_value)]
    for _ in range(1, CHEB):
        rho_next = 1.0 / (2.0 * spread_ratio - rho_prev)
        weights.append((rho_next * rho_prev, 2.0 * rho_next / half_width))
        rho_prev = rho_next
    return weights


def factors(s):
    poly = np.polynomial.Polynomial
    x, d, one, m = poly([0.0]), poly([0.0]), poly([1.0]), poly([0.0, 1.0])
    for keep, new in cheb_weights(s):
        d = keep * d + new * (one - m * x)
        x = x + d
    lead = x.coef[5]
    roots = x.roots()
    real = [r.real for r in roots if abs(r.imag) < 1e-9]
    pairs = sorted((r.real, r.imag) for r in roots if r.imag > 1e-9)
    assert lead < 0 and len(real) == 1 and len(pairs) == 2
    kap = (-lead * s**6) ** (1.0 / 6.0)
    shifts = [0.0, kap * (1.0 - real[0]) / s] + [kap * (1.0 - p[0]) / s for p in pairs]
    betas = [(kap * p[1] / s) ** 2 for p in pairs]
    return float(kap), [float(v) for v in shifts], [float(v) for v in betas]


def sroll(x, by):
    return pltpu.roll(x, by % 8, 0)


def lroll(x, by):
    return pltpu.roll(x, by % 128, 1)


def put(buf, i, v, val):
    buf[i, v + 2] = val
    if v >= 2:
        buf[i, v - 2] = lroll(val, 1)
    else:
        buf[i, v + 6] = lroll(val, -1)


def pair(src, fx, fy, d_one, d_two, beta, source, emit):
    held, mid = {}, {}

    def y(i, c):
        if (i, c) not in held:
            if i == -1:
                held[i, c] = sroll(y(7, c), 1)
            elif i == 8:
                held[i, c] = sroll(y(0, c), -1)
            else:
                held[i, c] = src[i, c + 2]
        return held[i, c]

    def w(i, c):
        if (i, c) not in mid:
            mid[i, c] = sroll(mid[7, c], 1) if i == -1 else sroll(mid[0, c], -1)
        return mid[i, c]

    def apply(f, d, i, c):
        k = c + 1
        up_down = (d[i, k] * f(i, c) + fy[i, k] * f(i - 1, c)) + fy[i + 1, k] * f(i + 1, c)
        return up_down + (fx[i, k] * f(i, c - 1) + fx[i, k + 1] * f(i, c + 1))

    first, second = set(), set()
    for i in range(8):
        for c in range(-1, 5):
            val = apply(y, d_one, i, c)
            if source is not None:
                val = val + source(i, c)
            mid[i, c] = val
        first.add(i)
        for j in range(8):
            if j not in second and {(j - 1) % 8, j, (j + 1) % 8} <= first:
                for v in (0, 3, 1, 2):
                    val = apply(w, d_two, j, v)
                    if beta is not None:
                        val = val + beta * src[j, v + 2]
                    emit(j, v, val)
                second.add(j)


def solve(buf, tmp, coefs, betas, source, emit):
    fx, fy, d = coefs
    pair(buf, fx, fy, d.at[0], d.at[1], None, source, functools.partial(put, tmp.at[0]))
    pair(tmp.at[0], fx, fy, d.at[2], d.at[2], betas[0], None, functools.partial(put, tmp.at[1]))
    pair(tmp.at[1], fx, fy, d.at[3], d.at[3], betas[1], None, emit)


def move_columns(x, table):
    high = x.astype(jnp.bfloat16)
    rest = x - high.astype(jnp.float32)
    middle = rest.astype(jnp.bfloat16)
    low = (rest - middle.astype(jnp.float32)).astype(jnp.bfloat16)
    stacked = jnp.concatenate([high, middle, low], 0)
    out = jnp.dot(stacked, table, preferred_element_type=jnp.float32)
    n = x.shape[0]
    return (out[:n] + out[n : 2 * n]) + out[2 * n :]


def kernel(
    n_t, fine_set, coarse_set,
    states, start, control, kappa, out,
    nat, xp, table_in, table_out, kp, fx0, fy0, c0, fxf, fyf, df, fxc, fyc, dc,
    g, ub, tmp, old, wd, rb, nb, lb, dp, eb, fb, lbuf, es, nat_f, nat_c,
    ss, rs, ls, lrecv, esend, esend_two, credit, go,
):
    t = lax.axis_index("tm")
    c = lax.axis_index("space")
    last = n_t - 1
    central = jnp.logical_and(t == last, c == 0)
    pairs = n_t // 2
    p = t // 2
    even = t % 2 == 0
    raw_slot, zero_slot, pair_slot = pairs - 1, pairs, pairs + 1
    partner = (t, 1 - c)
    right = (t + 1, 0 * c)
    hub = (0 * t + last, 0 * c)
    mine = pl.multiple_of(c * HALF, HALF)
    theirs = pl.multiple_of((1 - c) * HALF, HALF)

    def remote(src, dst, k, dev):
        return pltpu.make_async_remote_copy(
            src_ref=src, dst_ref=dst, send_sem=ss.at[k], recv_sem=rs.at[k], device_id=dev, device_id_type=MESH
        )

    barrier = pltpu.get_barrier_semaphore()
    pl.semaphore_signal(barrier, inc=1, device_id=partner, device_id_type=MESH)

    @pl.when(jnp.logical_and(c == 0, t > 0))
    def _():
        pl.semaphore_signal(barrier, inc=1, device_id=(t - 1, 0 * c), device_id_type=MESH)
        pl.semaphore_signal(barrier, inc=1, device_id=(t - 1, 0 * c + 1), device_id_type=MESH)

    @pl.when(jnp.logical_and(c == 0, t < last))
    def _():
        pl.semaphore_signal(barrier, inc=1, device_id=hub, device_id_type=MESH)

    def local(src, dst, k):
        return pltpu.make_async_copy(src, dst, ls.at[k])

    own_control = local(control.at[pl.ds(4 * c, 4)], nat.at[pl.ds(0, 4), pl.ds(mine, HALF), :], 0)
    own_kappa = local(kappa, nat.at[6, pl.ds(mine, HALF), :], 1)
    own_first = local(states.at[3], nat.at[5, pl.ds(mine, HALF), :], 2)
    own_start = local(start, nat.at[4, pl.ds(mine, HALF), :], 3)
    own_root = local(states.at[3], nat.at[4, pl.ds(mine, HALF), :], 2)
    own_next = local(states.at[7], nat.at[5, pl.ds(mine, HALF), :], 3)
    own_kappa.start()
    own_control.start()

    @pl.when(c == 0)
    def _():
        own_first.start()

        @pl.when(t == 0)
        def _():
            own_start.start()

    @pl.when(c == 1)
    def _():
        own_root.start()
        own_next.start()

    down = lax.broadcasted_iota(jnp.int32, (COLS, COLS), 0)
    across = lax.broadcasted_iota(jnp.int32, (COLS, COLS), 1)
    table_in[...] = jnp.where(down == 4 * (across % 128) + across // 128, 1.0, 0.0).astype(jnp.bfloat16)
    table_out[...] = jnp.where(across == 4 * (down % 128) + down // 128, 1.0, 0.0).astype(jnp.bfloat16)

    pl.semaphore_wait(barrier, 1 + jnp.where(t < last, 1, 0) + jnp.where(central, last, 0))

    to_control = remote(control.at[pl.ds(4 * (1 - c), 4)], nat.at[pl.ds(0, 4), pl.ds(mine, HALF), :], 0, partner)
    to_kappa = remote(kappa, nat.at[6, pl.ds(mine, HALF), :], 3, partner)
    to_root = remote(states.at[3], nat.at[4, pl.ds(mine, HALF), :], 1, partner)
    to_next = remote(states.at[7], nat.at[5, pl.ds(mine, HALF), :], 2, partner)
    to_first = remote(states.at[3], nat.at[5, pl.ds(mine, HALF), :], 2, partner)
    to_start = remote(start, nat.at[4, pl.ds(mine, HALF), :], 1, partner)
    to_right = [remote(states.at[7], nat.at[4, pl.ds(k * HALF, HALF), :], 5 + k, right) for k in range(2)]

    for k in range(2):

        @pl.when(jnp.logical_and(t < last, c == k))
        def _():
            to_right[k].start()

    to_kappa.start()

    @pl.when(c == 0)
    def _():
        to_root.start()
        to_next.start()

    @pl.when(c == 1)
    def _():
        to_first.start()

        @pl.when(t == 0)
        def _():
            to_start.start()

    to_control.start()

    @pl.when(central)
    def _():
        def give(k, carry):
            pl.semaphore_signal(credit, inc=1, device_id=(k, 0 * c), device_id_type=MESH)
            return carry

        give(0, 0)
        lax.fori_loop(0, min(WINDOW, pairs - 1), lambda k, carry: give(2 * k + 1, carry), 0)

    def to_layout(x, use):
        moved = move_columns(x, table_in[...])
        for v in range(4):
            xp[v] = moved[:, 128 * v : 128 * (v + 1)]
        for i in range(8):
            for v in range(4):
                use(i, v, xp[v, pl.ds(i, 8, stride=8), :])

    def from_layout(give):
        for i in range(8):
            for v in range(4):
                xp[v, pl.ds(i, 8, stride=8), :] = give(i, v)
        return move_columns(jnp.concatenate([xp[v] for v in range(4)], 1), table_out[...])

    own_kappa.wait()
    to_kappa.wait()

    def hold_kappa(i, v, val):
        kp[i, v] = val

    to_layout(nat[6], hold_kappa)
    lane = lax.broadcasted_iota(jnp.int32, (8, 128), 1)
    sub = lax.broadcasted_iota(jnp.int32, (8, 128), 0)
    zero = jnp.zeros((8, 128), jnp.float32)
    for i in range(8):
        row = [kp[i, v] for v in range(4)]
        after = jnp.where(lane < 127, lroll(row[0], -1), zero)
        before = jnp.where(lane > 0, lroll(row[3], 1), zero)
        wide = [before] + row + [after]
        side = [0.5 * (wide[k] + wide[k + 1]) for k in range(5)]
        inner_right = jnp.where(lane < 127, side[4], zero)
        inner = [jnp.where(lane > 0, side[0], zero), side[1], side[2], side[3], inner_right]
        for k in range(5):
            fx0[i, k + 1] = inner[k]
        fx0[i, 0] = lroll(side[3], 1)
        fx0[i, 6] = lroll(side[1], -1)
        for v in range(4):
            if i == 0:
                above = jnp.where(sub > 0, sroll(kp[7, v], 1), zero)
            else:
                above = kp[i - 1, v]
            if i == 7:
                below = jnp.where(sub < 7, sroll(kp[0, v], -1), zero)
            else:
                below = kp[i + 1, v]
            up = 0.5 * (above + row[v])
            low = 0.5 * (row[v] + below)
            centre = ((up + low) + side[v]) + side[v + 1]
            pieces = [(c0, i, centre), (fy0, i, jnp.where(sub > 0, up, zero) if i == 0 else up)]
            if i == 7:
                pieces.append((fy0, 8, jnp.where(sub < 7, low, zero)))
            for ref, at, val in pieces:
                ref[at, v + 1] = val
                if v == 3:
                    ref[at, 0] = lroll(val, 1)
                if v == 0:
                    ref[at, 5] = lroll(val, -1)

    def fill(kap, shifts, fx, fy, d):
        fx[...] = fx0[...] * (-kap)
        fy[...] = fy0[...] * (-kap)
        for k in range(4):
            d[k] = c0[...] * kap + shifts[k]

    fill(fine_set[0], fine_set[1], fxf, fyf, df)

    @pl.when(c == 0)
    def _():
        own_first.wait()
        to_first.wait_recv()

        @pl.when(t == 0)
        def _():
            own_start.wait()
            to_start.wait_recv()

        @pl.when(t > 0)
        def _():
            to_right[0].wait_recv()
            to_right[1].wait_recv()

    @pl.when(c == 1)
    def _():
        own_root.wait()
        own_next.wait()
        to_root.wait_recv()
        to_next.wait_recv()

    to_layout(nat[4], functools.partial(put, ub))

    def hold_old(i, v, val):
        old[i, v] = val

    to_layout(nat[5], hold_old)
    own_control.wait()
    to_control.wait()

    def bring(j, carry):
        def hold(i, v, val):
            val = val * (-fine_set[0])
            g[j, i, v + 1] = val
            if v == 3:
                g[j, i, 0] = lroll(val, 1)
            if v == 0:
                g[j, i, 5] = lroll(val, -1)

        to_layout(nat[j], hold)
        return carry

    lax.fori_loop(0, 4, bring, 0)
    g[4] = jnp.zeros(g.shape[1:], jnp.float32)

    def fine(j, carry):
        @pl.when(j == 4)
        def _():
            for i in range(8):
                for v in range(4):
                    put(ub, i, v, wd[3, i, v] - old[i, v])

        source = g.at[jnp.minimum(j, 4)]

        def emit(i, v, val):
            val = val + ub[i, v + 2]
            put(ub, i, v, val)
            wd[j, i, v] = val

        solve(ub, tmp, (fxf, fyf, df), fine_set[2], lambda i, k: source[i, k + 1], emit)
        return carry

    lax.fori_loop(0, 8, fine, 0)

    to_r = remote(wd.at[7], rb, 7, partner)
    to_c = remote(wd.at[3], nb, 8, partner)
    to_d_partner = remote(wd.at[pl.ds(4, 3)], dp, 9, partner)
    to_d_right = remote(wd.at[pl.ds(4, 3)], dp, 9, right)

    def to_hub(src, slot):
        return pltpu.make_async_remote_copy(
            src_ref=src, dst_ref=lbuf.at[slot], send_sem=ss.at[13], recv_sem=lrecv.at[slot],
            device_id=hub, device_id_type=MESH,
        )

    to_second = pltpu.make_async_remote_copy(
        src_ref=lb, dst_ref=lbuf.at[pair_slot], send_sem=ss.at[15], recv_sem=lrecv.at[pair_slot],
        device_id=right, device_id_type=MESH,
    )

    @pl.when(c == 1)
    def _():
        @pl.when(t < last)
        def _():
            to_r.start()

        to_c.start()

        @pl.when(even)
        def _():
            pl.semaphore_wait(go, 1)

        @pl.when(t < last)
        def _():
            to_d_right.start()

    fill(coarse_set[0], coarse_set[1], fxc, fyc, dc)
    coarse = (fxc, fyc, dc)

    def coarse_solve(emit):
        solve(ub, tmp, coarse, coarse_set[2], None, emit)

    def load(ref):
        for i in range(8):
            for v in range(4):
                put(ub, i, v, ref[i, v])

    def advance(n):
        def one(k, carry):
            coarse_solve(lambda i, v, val: put(ub, i, v, val + ub[i, v + 2]))
            return carry

        lax.fori_loop(0, n, one, 0)

    def add(dst, other):
        for i in range(8):
            for v in range(4):
                dst[i, v] = ub[i, v + 2] + other[i, v]

    @pl.when(jnp.logical_and(c == 0, t < last))
    def _():
        advance(1)
        to_r.wait_recv()
        add(lb, rb)

        @pl.when(even)
        def _():
            to_second.start()

            @pl.when(t == 0)
            def _():
                pl.semaphore_wait(credit, 1)
                to_hub(lb, raw_slot).start()

            to_second.wait_send()
            pl.semaphore_signal(go, inc=1, device_id=partner, device_id_type=MESH)

        @pl.when(jnp.logical_not(even))
        def _():
            @pl.when(t > 1)
            def _():
                to_second.wait_recv()
                load(lbuf.at[pair_slot])
                advance(2)
                add(lb, lb)

            pl.semaphore_wait(credit, 1)
            to_hub(lb, p).start()

    @pl.when(c == 0)
    def _():
        to_d_partner.start()

    to_out_f = remote(
        nat_f.at[:, pl.ds(theirs, HALF), :], out.at[pl.ds(4 * c, 3)], 10, partner
    )

    own_out_f = local(nat_f.at[:, pl.ds(mine, HALF), :], out.at[pl.ds(4 * c, 3)], 0)

    def f_points():
        has = jnp.logical_or(c == 1, t > 0)

        @pl.when(has)
        def _():
            to_d_partner.wait_recv()

        @pl.when(jnp.logical_not(has))
        def _():
            dp[...] = jnp.zeros(dp.shape, jnp.float32)

        def one(j, carry):
            nat_f[j] = from_layout(lambda i, v: wd[j, i, v] + dp[j, i, v])
            return carry

        lax.fori_loop(0, 3, one, 0)
        to_out_f.start()
        own_out_f.start()

    @pl.when(jnp.logical_not(central))
    def _():
        f_points()

    def to_owner(q):
        return pltpu.make_async_remote_copy(
            src_ref=es.at[q], dst_ref=eb, send_sem=esend.at[q], recv_sem=rs.at[14],
            device_id=(2 * q, 0 * c), device_id_type=MESH,
        )

    def to_odd(q):
        return pltpu.make_async_remote_copy(
            src_ref=es.at[q], dst_ref=eb, send_sem=esend_two.at[q], recv_sem=rs.at[14],
            device_id=(2 * q + 1, 0 * c), device_id_type=MESH,
        )

    forward = pltpu.make_async_remote_copy(
        src_ref=eb, dst_ref=eb, send_sem=ss.at[16], recv_sem=rs.at[14], device_id=right, device_id_type=MESH
    )
    direct_from = max(1, pairs - DIRECT)

    @pl.when(central)
    def _():
        lbuf[zero_slot] = jnp.zeros(GRID, jnp.float32)
        to_hub(lb, raw_slot).wait_recv()
        load(lbuf.at[raw_slot])

        def turn(k, carry):
            odd = k % 2 == 1
            q = k // 2
            final = k == last - 1

            @pl.when(jnp.logical_and(odd, q + WINDOW < pairs - 1))
            def _():
                pl.semaphore_signal(credit, inc=1, device_id=(2 * (q + WINDOW) + 1, 0 * c), device_id_type=MESH)

            @pl.when(k == min(10, last - 1))
            def _():
                f_points()

            coarse_solve(lambda i, v, val: put(ub, i, v, val + ub[i, v + 2]))

            @pl.when(odd)
            def _():
                to_hub(lb, q).wait_recv()

            @pl.when(final)
            def _():
                to_second.wait_recv()

            added = lbuf.at[jnp.where(odd, q, jnp.where(final, pair_slot, zero_slot))]
            kept = es.at[jnp.where(odd, q + 1, 0)]

            def emit(i, v, val):
                val = val + (ub[i, v + 2] + added[i, v])
                put(ub, i, v, val)
                kept[i, v] = val

            coarse_solve(emit)

            @pl.when(odd)
            def _():
                to_owner(q + 1).start()

                @pl.when(jnp.logical_and(q + 1 >= direct_from, q + 1 < pairs - 1))
                def _():
                    to_odd(q + 1).start()

                @pl.when(q >= 4)
                def _():
                    to_owner(q - 3).wait_send()

            return carry

        lax.fori_loop(1, last, turn, 0)
        eb[...] = es[0]

    to_out_c = [
        remote(nat_c.at[k, pl.ds(HALF, HALF), :], out.at[4 * k + 3], 11 + k, partner) for k in range(2)
    ]

    own_out_c = [local(nat_c.at[k, pl.ds(0, HALF), :], out.at[4 * k + 3], 1 + k) for k in range(2)]

    @pl.when(c == 0)
    def _():
        to_c.wait_recv()

        @pl.when(t == 0)
        def _():
            eb[...] = jnp.zeros(eb.shape, jnp.float32)

        @pl.when(t == 1)
        def _():
            to_second.wait_recv()
            eb[...] = lbuf[pair_slot]

        @pl.when(jnp.logical_and(t > 1, t < last))
        def _():
            to_owner(0).wait_recv()

        @pl.when(jnp.logical_and(even, jnp.logical_and(p > 0, p < direct_from)))
        def _():
            forward.start()

        @pl.when(t < last)
        def _():
            load(eb)

        @pl.when(jnp.logical_and(jnp.logical_not(even), jnp.logical_and(t > 1, t < last)))
        def _():
            advance(2)
            add(eb, lbuf.at[pair_slot])
            load(eb)

        nat_c[0] = from_layout(lambda i, v: wd[3, i, v] + eb[i, v])
        to_out_c[0].start()
        own_out_c[0].start()

        def emit(i, v, val):
            fb[i, v] = (val + ub[i, v + 2]) + wd[7, i, v]

        coarse_solve(emit)
        nat_c[1] = from_layout(lambda i, v: nb[i, v] + fb[i, v])
        to_out_c[1].start()
        own_out_c[1].start()
        own_out_c[0].wait()
        own_out_c[1].wait()

        @pl.when(jnp.logical_and(even, jnp.logical_and(p > 0, p < direct_from)))
        def _():
            forward.wait_send()

    @pl.when(c == 1)
    def _():
        to_out_c[0].wait_recv()
        to_out_c[1].wait_recv()
        to_c.wait_send()
        to_first.wait_send()

        @pl.when(t == 0)
        def _():
            to_start.wait_send()

        @pl.when(t < last)
        def _():
            to_r.wait_send()
            to_d_right.wait_send()

    to_out_f.wait()
    own_out_f.wait()
    for k in range(2):

        @pl.when(jnp.logical_and(t < last, c == k))
        def _():
            to_right[k].wait_send()

    @pl.when(c == 0)
    def _():
        to_out_c[0].wait_send()
        to_out_c[1].wait_send()
        to_root.wait_send()
        to_next.wait_send()
        to_d_partner.wait_send()

        @pl.when(jnp.logical_or(t == 0, jnp.logical_and(jnp.logical_not(even), t < last)))
        def _():
            to_hub(lb, p).wait_send()

    @pl.when(central)
    def _():
        def drain(q, carry):
            to_owner(q).wait_send()
            return carry

        def drain_two(q, carry):
            to_odd(q).wait_send()
            return carry

        lax.fori_loop(max(1, pairs - 4), pairs, drain, 0)
        lax.fori_loop(direct_from, pairs - 1, drain_two, 0)


def solution(mesh):
    n_t = mesh.shape["tm"]
    fine_set = factors(step_size)
    coarse_set = factors(FACTOR * step_size)
    f32 = jnp.float32

    def vmem(*shape):
        return pltpu.VMEM(shape, f32)

    def on_device(states, start, control, kappa):
        tile = (8, 128)
        return pl.pallas_call(
            functools.partial(kernel, n_t, fine_set, coarse_set),
            out_shape=jax.ShapeDtypeStruct((8, HALF, COLS), f32),
            in_specs=[pl.BlockSpec(memory_space=pl.ANY)] * 4,
            out_specs=pl.BlockSpec(memory_space=pl.ANY),
            scratch_shapes=[
                vmem(7, ROWS, COLS),
                vmem(4, ROWS, 128),
                pltpu.VMEM((COLS, COLS), jnp.bfloat16),
                pltpu.VMEM((COLS, COLS), jnp.bfloat16),
                vmem(*GRID),
                vmem(8, 7, *tile), vmem(9, 6, *tile), vmem(8, 6, *tile),
                vmem(8, 7, *tile), vmem(9, 6, *tile), vmem(4, 8, 6, *tile),
                vmem(8, 7, *tile), vmem(9, 6, *tile), vmem(4, 8, 6, *tile),
                vmem(5, 8, 6, *tile),
                vmem(8, 8, *tile),
                vmem(2, 8, 8, *tile),
                vmem(*GRID),
                vmem(8, *GRID),
                vmem(*GRID), vmem(*GRID), vmem(*GRID),
                vmem(3, *GRID),
                vmem(*GRID), vmem(*GRID),
                vmem(n_t // 2 + 2, *GRID),
                vmem(n_t // 2, *GRID),
                vmem(3, ROWS, COLS),
                vmem(2, ROWS, COLS),
                pltpu.SemaphoreType.DMA((17,)),
                pltpu.SemaphoreType.DMA((17,)),
                pltpu.SemaphoreType.DMA((4,)),
                pltpu.SemaphoreType.DMA((n_t,)),
                pltpu.SemaphoreType.DMA((n_t,)),
                pltpu.SemaphoreType.DMA((n_t,)),
                pltpu.SemaphoreType.REGULAR,
                pltpu.SemaphoreType.REGULAR,
            ],
            compiler_params=pltpu.CompilerParams(
                collective_id=0, has_side_effects=True, vmem_limit_bytes=48 * 2**20
            ),
        )(states, start, control, kappa)

    return jax.shard_map(
        on_device,
        mesh=mesh,
        in_specs=(P("tm", "space", None), P("space", None), P("tm", "space", None), P("space", None)),
        out_specs=P("tm", "space", None),
        check_vma=False,
    )
```

```python
import functools

import jax
import jax.numpy as jnp
import numpy as np
from jax import lax
from jax.experimental import pallas as pl
from jax.experimental.pallas import tpu as pltpu
from jax.sharding import PartitionSpec as P

MESH = pl.DeviceIdType.MESH
CHEB = 6
FACTOR = 4
step_size = 0.1
kappa_top = 1.25
ROWS = 64
COLS = 512
HALF = ROWS // 2
WINDOW = 9
DIRECT = 4
GRID = (8, 4, 8, 128)


def cheb_weights(step_scale):
    highest = 1.0 + 8.0 * step_scale * kappa_top
    centre_value = 0.5 * (highest + 1.0)
    half_width = 0.5 * (highest - 1.0)
    spread_ratio = centre_value / half_width
    rho_prev = 1.0 / spread_ratio
    weights = [(0.0, 1.0 / centre_value)]
    for _ in range(1, CHEB):
        rho_next = 1.0 / (2.0 * spread_ratio - rho_prev)
        weights.append((rho_next * rho_prev, 2.0 * rho_next / half_width))
        rho_prev = rho_next
    return weights


def factors(s):
    poly = np.polynomial.Polynomial
    x, d, one, m = poly([0.0]), poly([0.0]), poly([1.0]), poly([0.0, 1.0])
    for keep, new in cheb_weights(s):
        d = keep * d + new * (one - m * x)
        x = x + d
    lead = x.coef[5]
    roots = x.roots()
    real = [r.real for r in roots if abs(r.imag) < 1e-9]
    pairs = sorted((r.real, r.imag) for r in roots if r.imag > 1e-9)
    assert lead < 0 and len(real) == 1 and len(pairs) == 2
    kap = (-lead * s**6) ** (1.0 / 6.0)
    shifts = [0.0, kap * (1.0 - real[0]) / s] + [kap * (1.0 - p[0]) / s for p in pairs]
    betas = [(kap * p[1] / s) ** 2 for p in pairs]
    return float(kap), [float(v) for v in shifts], [float(v) for v in betas]


def sroll(x, by):
    return pltpu.roll(x, by % 8, 0)


def lroll(x, by):
    return pltpu.roll(x, by % 128, 1)


def put(buf, i, v, val):
    buf[i, v + 2] = val
    if v >= 2:
        buf[i, v - 2] = lroll(val, 1)
    else:
        buf[i, v + 6] = lroll(val, -1)


def pair(src, fx, fy, d_one, d_two, beta, source, emit):
    held, mid = {}, {}

    def y(i, c):
        if (i, c) not in held:
            if i == -1:
                held[i, c] = sroll(y(7, c), 1)
            elif i == 8:
                held[i, c] = sroll(y(0, c), -1)
            else:
                held[i, c] = src[i, c + 2]
        return held[i, c]

    def w(i, c):
        if (i, c) not in mid:
            mid[i, c] = sroll(mid[7, c], 1) if i == -1 else sroll(mid[0, c], -1)
        return mid[i, c]

    def apply(f, d, i, c):
        k = c + 1
        up_down = (d[i, k] * f(i, c) + fy[i, k] * f(i - 1, c)) + fy[i + 1, k] * f(i + 1, c)
        return up_down + (fx[i, k] * f(i, c - 1) + fx[i, k + 1] * f(i, c + 1))

    first, second = set(), set()
    for i in range(8):
        for c in range(-1, 5):
            val = apply(y, d_one, i, c)
            if source is not None:
                val = val + source(i, c)
            mid[i, c] = val
        first.add(i)
        for j in range(8):
            if j not in second and {(j - 1) % 8, j, (j + 1) % 8} <= first:
                for v in (0, 3, 1, 2):
                    val = apply(w, d_two, j, v)
                    if beta is not None:
                        val = val + beta * src[j, v + 2]
                    emit(j, v, val)
                second.add(j)


def solve(buf, tmp, coefs, betas, source, emit):
    fx, fy, d = coefs
    pair(buf, fx, fy, d.at[0], d.at[1], None, source, functools.partial(put, tmp.at[0]))
    pair(tmp.at[0], fx, fy, d.at[2], d.at[2], betas[0], None, functools.partial(put, tmp.at[1]))
    pair(tmp.at[1], fx, fy, d.at[3], d.at[3], betas[1], None, emit)


def move_columns(x, table):
    high = x.astype(jnp.bfloat16)
    rest = x - high.astype(jnp.float32)
    middle = rest.astype(jnp.bfloat16)
    low = (rest - middle.astype(jnp.float32)).astype(jnp.bfloat16)
    stacked = jnp.concatenate([high, middle, low], 0)
    out = jnp.dot(stacked, table, preferred_element_type=jnp.float32)
    n = x.shape[0]
    return (out[:n] + out[n : 2 * n]) + out[2 * n :]


def kernel(
    n_t, fine_set, coarse_set,
    states, start, control, kappa, out,
    nat, xp, table_in, table_out, kp, fx0, fy0, c0, fxf, fyf, df, fxc, fyc, dc,
    g, ub, tmp, old, wd, rb, nb, lb, dp, eb, fb, lbuf, es, nat_f, nat_c,
    ss, rs, ls, lrecv, esend, esend_two, credit, go,
):
    t = lax.axis_index("tm")
    c = lax.axis_index("space")
    last = n_t - 1
    central = jnp.logical_and(t == last, c == 0)
    pairs = n_t // 2
    p = t // 2
    even = t % 2 == 0
    raw_slot, pair_slot = pairs - 1, pairs
    partner = (t, 1 - c)
    right = (t + 1, 0 * c)
    hub = (0 * t + last, 0 * c)
    mine = pl.multiple_of(c * HALF, HALF)
    theirs = pl.multiple_of((1 - c) * HALF, HALF)

    def remote(src, dst, k, dev):
        return pltpu.make_async_remote_copy(
            src_ref=src, dst_ref=dst, send_sem=ss.at[k], recv_sem=rs.at[k], device_id=dev, device_id_type=MESH
        )

    barrier = pltpu.get_barrier_semaphore()
    pl.semaphore_signal(barrier, inc=1, device_id=partner, device_id_type=MESH)

    @pl.when(jnp.logical_and(c == 0, t > 0))
    def _():
        pl.semaphore_signal(barrier, inc=1, device_id=(t - 1, 0 * c), device_id_type=MESH)
        pl.semaphore_signal(barrier, inc=1, device_id=(t - 1, 0 * c + 1), device_id_type=MESH)

    @pl.when(jnp.logical_and(c == 0, t < last))
    def _():
        pl.semaphore_signal(barrier, inc=1, device_id=hub, device_id_type=MESH)

    def local(src, dst, k):
        return pltpu.make_async_copy(src, dst, ls.at[k])

    own_control = local(control.at[pl.ds(4 * c, 4)], nat.at[pl.ds(0, 4), pl.ds(mine, HALF), :], 0)
    own_kappa = local(kappa, nat.at[6, pl.ds(mine, HALF), :], 1)
    own_first = local(states.at[3], nat.at[5, pl.ds(mine, HALF), :], 2)
    own_start = local(start, nat.at[4, pl.ds(mine, HALF), :], 3)
    own_root = local(states.at[3], nat.at[4, pl.ds(mine, HALF), :], 2)
    own_next = local(states.at[7], nat.at[5, pl.ds(mine, HALF), :], 3)
    own_kappa.start()
    own_control.start()

    @pl.when(c == 0)
    def _():
        own_first.start()

        @pl.when(t == 0)
        def _():
            own_start.start()

    @pl.when(c == 1)
    def _():
        own_root.start()
        own_next.start()

    down = lax.broadcasted_iota(jnp.int32, (COLS, COLS), 0)
    across = lax.broadcasted_iota(jnp.int32, (COLS, COLS), 1)
    table_in[...] = jnp.where(down == 4 * (across % 128) + across // 128, 1.0, 0.0).astype(jnp.bfloat16)
    table_out[...] = jnp.where(across == 4 * (down % 128) + down // 128, 1.0, 0.0).astype(jnp.bfloat16)

    pl.semaphore_wait(barrier, 1 + jnp.where(t < last, 1, 0) + jnp.where(central, last, 0))

    to_control = remote(control.at[pl.ds(4 * (1 - c), 4)], nat.at[pl.ds(0, 4), pl.ds(mine, HALF), :], 0, partner)
    to_kappa = remote(kappa, nat.at[6, pl.ds(mine, HALF), :], 3, partner)
    to_root = remote(states.at[3], nat.at[4, pl.ds(mine, HALF), :], 1, partner)
    to_next = remote(states.at[7], nat.at[5, pl.ds(mine, HALF), :], 2, partner)
    to_first = remote(states.at[3], nat.at[5, pl.ds(mine, HALF), :], 2, partner)
    to_start = remote(start, nat.at[4, pl.ds(mine, HALF), :], 1, partner)
    to_right = [remote(states.at[7], nat.at[4, pl.ds(k * HALF, HALF), :], 5 + k, right) for k in range(2)]

    for k in range(2):

        @pl.when(jnp.logical_and(t < last, c == k))
        def _():
            to_right[k].start()

    to_kappa.start()

    @pl.when(c == 0)
    def _():
        to_root.start()
        to_next.start()

    @pl.when(c == 1)
    def _():
        to_first.start()

        @pl.when(t == 0)
        def _():
            to_start.start()

    to_control.start()

    @pl.when(central)
    def _():
        def give(k, carry):
            pl.semaphore_signal(credit, inc=1, device_id=(k, 0 * c), device_id_type=MESH)
            return carry

        give(0, 0)
        lax.fori_loop(0, min(WINDOW, pairs - 1), lambda k, carry: give(2 * k + 1, carry), 0)

    def to_layout(x, at, use):
        moved = move_columns(x, table_in[...])
        for v in range(4):
            xp[at, v] = moved[:, 128 * v : 128 * (v + 1)]
        for i in range(8):
            for v in range(4):
                use(i, v, xp[at, v, pl.ds(i, 8, stride=8), :])

    def from_layout(at, give):
        for i in range(8):
            for v in range(4):
                xp[at, v, pl.ds(i, 8, stride=8), :] = give(i, v)
        return move_columns(jnp.concatenate([xp[at, v] for v in range(4)], 1), table_out[...])

    own_kappa.wait()
    to_kappa.wait()

    def hold_kappa(i, v, val):
        kp[i, v] = val

    to_layout(nat[6], 0, hold_kappa)
    lane = lax.broadcasted_iota(jnp.int32, (8, 128), 1)
    sub = lax.broadcasted_iota(jnp.int32, (8, 128), 0)
    zero = jnp.zeros((8, 128), jnp.float32)
    for i in range(8):
        row = [kp[i, v] for v in range(4)]
        after = jnp.where(lane < 127, lroll(row[0], -1), zero)
        before = jnp.where(lane > 0, lroll(row[3], 1), zero)
        wide = [before] + row + [after]
        side = [0.5 * (wide[k] + wide[k + 1]) for k in range(5)]
        inner_right = jnp.where(lane < 127, side[4], zero)
        inner = [jnp.where(lane > 0, side[0], zero), side[1], side[2], side[3], inner_right]
        for k in range(5):
            fx0[i, k + 1] = inner[k]
        fx0[i, 0] = lroll(side[3], 1)
        fx0[i, 6] = lroll(side[1], -1)
        for v in range(4):
            if i == 0:
                above = jnp.where(sub > 0, sroll(kp[7, v], 1), zero)
            else:
                above = kp[i - 1, v]
            if i == 7:
                below = jnp.where(sub < 7, sroll(kp[0, v], -1), zero)
            else:
                below = kp[i + 1, v]
            up = 0.5 * (above + row[v])
            low = 0.5 * (row[v] + below)
            centre = ((up + low) + side[v]) + side[v + 1]
            pieces = [(c0, i, centre), (fy0, i, jnp.where(sub > 0, up, zero) if i == 0 else up)]
            if i == 7:
                pieces.append((fy0, 8, jnp.where(sub < 7, low, zero)))
            for ref, at, val in pieces:
                ref[at, v + 1] = val
                if v == 3:
                    ref[at, 0] = lroll(val, 1)
                if v == 0:
                    ref[at, 5] = lroll(val, -1)

    def fill(kap, shifts, fx, fy, d):
        fx[...] = fx0[...] * (-kap)
        fy[...] = fy0[...] * (-kap)
        for k in range(4):
            d[k] = c0[...] * kap + shifts[k]

    fill(fine_set[0], fine_set[1], fxf, fyf, df)
    fill(coarse_set[0], coarse_set[1], fxc, fyc, dc)

    @pl.when(c == 0)
    def _():
        own_first.wait()
        to_first.wait_recv()

        @pl.when(t == 0)
        def _():
            own_start.wait()
            to_start.wait_recv()

        @pl.when(t > 0)
        def _():
            to_right[0].wait_recv()
            to_right[1].wait_recv()

    @pl.when(c == 1)
    def _():
        own_root.wait()
        own_next.wait()
        to_root.wait_recv()
        to_next.wait_recv()

    to_layout(nat[4], 0, functools.partial(put, ub))

    def hold_old(i, v, val):
        old[i, v] = val

    to_layout(nat[5], 1, hold_old)
    own_control.wait()
    to_control.wait()

    def hold_source(j, i, v, val):
        val = val * (-fine_set[0])
        g[j, i, v + 1] = val
        if v == 3:
            g[j, i, 0] = lroll(val, 1)
        if v == 0:
            g[j, i, 5] = lroll(val, -1)

    for j in range(4):
        to_layout(nat[j], j, functools.partial(hold_source, j))
    g[4] = jnp.zeros(g.shape[1:], jnp.float32)

    def fine(j, carry):
        @pl.when(j == 4)
        def _():
            for i in range(8):
                for v in range(4):
                    put(ub, i, v, wd[3, i, v] - old[i, v])

        source = g.at[jnp.minimum(j, 4)]

        def emit(i, v, val):
            val = val + ub[i, v + 2]
            put(ub, i, v, val)
            wd[j, i, v] = val

        solve(ub, tmp, (fxf, fyf, df), fine_set[2], lambda i, k: source[i, k + 1], emit)
        return carry

    lax.fori_loop(0, 8, fine, 0)

    to_r = remote(wd.at[7], rb, 7, partner)
    to_c = remote(wd.at[3], nb, 8, partner)
    to_d_partner = remote(wd.at[pl.ds(4, 3)], dp, 9, partner)
    to_d_right = remote(wd.at[pl.ds(4, 3)], dp, 9, right)

    def to_hub(src, slot):
        return pltpu.make_async_remote_copy(
            src_ref=src, dst_ref=lbuf.at[slot], send_sem=ss.at[13], recv_sem=lrecv.at[slot],
            device_id=hub, device_id_type=MESH,
        )

    to_second = pltpu.make_async_remote_copy(
        src_ref=lb, dst_ref=lbuf.at[pair_slot], send_sem=ss.at[15], recv_sem=lrecv.at[pair_slot],
        device_id=right, device_id_type=MESH,
    )

    @pl.when(c == 1)
    def _():
        @pl.when(t < last)
        def _():
            to_r.start()

        to_c.start()

        @pl.when(even)
        def _():
            pl.semaphore_wait(go, 1)

        @pl.when(t < last)
        def _():
            to_d_right.start()

    coarse = (fxc, fyc, dc)

    def coarse_solve(emit):
        solve(ub, tmp, coarse, coarse_set[2], None, emit)

    def load(ref):
        for i in range(8):
            for v in range(4):
                put(ub, i, v, ref[i, v])

    def advance(n):
        def one(k, carry):
            coarse_solve(lambda i, v, val: put(ub, i, v, val + ub[i, v + 2]))
            return carry

        lax.fori_loop(0, n, one, 0)

    def add(dst, other):
        for i in range(8):
            for v in range(4):
                dst[i, v] = ub[i, v + 2] + other[i, v]

    @pl.when(jnp.logical_and(c == 0, t < last))
    def _():
        advance(1)
        to_r.wait_recv()
        add(lb, rb)

        @pl.when(even)
        def _():
            to_second.start()

            @pl.when(t == 0)
            def _():
                pl.semaphore_wait(credit, 1)
                to_hub(lb, raw_slot).start()

            to_second.wait_send()
            pl.semaphore_signal(go, inc=1, device_id=partner, device_id_type=MESH)

        @pl.when(jnp.logical_not(even))
        def _():
            @pl.when(t > 1)
            def _():
                to_second.wait_recv()
                load(lbuf.at[pair_slot])
                advance(2)
                add(lb, lb)

            pl.semaphore_wait(credit, 1)
            to_hub(lb, p).start()

    @pl.when(c == 0)
    def _():
        to_d_partner.start()

    to_out_f = remote(
        nat_f.at[:, pl.ds(theirs, HALF), :], out.at[pl.ds(4 * c, 3)], 10, partner
    )

    own_out_f = local(nat_f.at[:, pl.ds(mine, HALF), :], out.at[pl.ds(4 * c, 3)], 0)

    def f_points():
        has = jnp.logical_or(c == 1, t > 0)

        @pl.when(has)
        def _():
            to_d_partner.wait_recv()

        @pl.when(jnp.logical_not(has))
        def _():
            dp[...] = jnp.zeros(dp.shape, jnp.float32)

        for j in range(3):
            nat_f[j] = from_layout(j, lambda i, v: wd[j, i, v] + dp[j, i, v])
        to_out_f.start()
        own_out_f.start()

    @pl.when(jnp.logical_not(central))
    def _():
        f_points()

    def to_owner(q):
        return pltpu.make_async_remote_copy(
            src_ref=es.at[q], dst_ref=eb, send_sem=esend.at[q], recv_sem=rs.at[14],
            device_id=(2 * q, 0 * c), device_id_type=MESH,
        )

    def to_odd(q):
        return pltpu.make_async_remote_copy(
            src_ref=es.at[q], dst_ref=eb, send_sem=esend_two.at[q], recv_sem=rs.at[14],
            device_id=(2 * q + 1, 0 * c), device_id_type=MESH,
        )

    forward = pltpu.make_async_remote_copy(
        src_ref=eb, dst_ref=eb, send_sem=ss.at[16], recv_sem=rs.at[14], device_id=right, device_id_type=MESH
    )
    direct_from = max(1, pairs - DIRECT)

    @pl.when(central)
    def _():
        to_hub(lb, raw_slot).wait_recv()
        load(lbuf.at[raw_slot])

        def turns(n, added, kept):
            for k in range(n):
                if k < n - 1:
                    coarse_solve(lambda i, v, val: put(ub, i, v, val + ub[i, v + 2]))
                else:

                    def emit(i, v, val):
                        val = val + (ub[i, v + 2] + added[i, v])
                        put(ub, i, v, val)
                        kept[i, v] = val

                    coarse_solve(emit)

        def send(q):
            to_owner(q).start()

            @pl.when(jnp.logical_and(q >= direct_from, q < pairs - 1))
            def _():
                to_odd(q).start()

        to_hub(lb, 0).wait_recv()
        turns(2, lbuf.at[0], es.at[1])

        def turn(q, carry):
            send(q)

            @pl.when(q + WINDOW - 1 < pairs - 1)
            def _():
                pl.semaphore_signal(credit, inc=1, device_id=(2 * (q + WINDOW) - 1, 0 * c), device_id_type=MESH)

            @pl.when(q == min(5, pairs - 2))
            def _():
                f_points()

            @pl.when(q >= 5)
            def _():
                to_owner(q - 4).wait_send()

            to_hub(lb, q).wait_recv()
            turns(4, lbuf.at[q], es.at[q + 1])
            return carry

        lax.fori_loop(1, pairs - 1, turn, 0)
        send(pairs - 1)
        to_second.wait_recv()
        turns(2, lbuf.at[pair_slot], eb)

    to_out_c = [
        remote(nat_c.at[k, pl.ds(HALF, HALF), :], out.at[4 * k + 3], 11 + k, partner) for k in range(2)
    ]
    own_out_c = [local(nat_c.at[k, pl.ds(0, HALF), :], out.at[4 * k + 3], 1 + k) for k in range(2)]

    @pl.when(c == 0)
    def _():
        to_c.wait_recv()

        @pl.when(t == 0)
        def _():
            eb[...] = jnp.zeros(eb.shape, jnp.float32)

        @pl.when(t == 1)
        def _():
            to_second.wait_recv()
            eb[...] = lbuf[pair_slot]

        @pl.when(jnp.logical_and(t > 1, t < last))
        def _():
            to_owner(0).wait_recv()

        @pl.when(jnp.logical_and(even, jnp.logical_and(p > 0, p < direct_from)))
        def _():
            forward.start()

        @pl.when(t < last)
        def _():
            load(eb)

        @pl.when(jnp.logical_and(jnp.logical_not(even), jnp.logical_and(t > 1, t < last)))
        def _():
            advance(2)
            add(eb, lbuf.at[pair_slot])
            load(eb)

        nat_c[0] = from_layout(0, lambda i, v: wd[3, i, v] + eb[i, v])

        def emit(i, v, val):
            fb[i, v] = (val + ub[i, v + 2]) + wd[7, i, v]

        coarse_solve(emit)
        nat_c[1] = from_layout(1, lambda i, v: nb[i, v] + fb[i, v])
        for k in range(2):
            to_out_c[k].start()
            own_out_c[k].start()
        own_out_c[0].wait()
        own_out_c[1].wait()

        @pl.when(jnp.logical_and(even, jnp.logical_and(p > 0, p < direct_from)))
        def _():
            forward.wait_send()

    @pl.when(c == 1)
    def _():
        to_out_c[0].wait_recv()
        to_out_c[1].wait_recv()
        to_c.wait_send()
        to_first.wait_send()

        @pl.when(t == 0)
        def _():
            to_start.wait_send()

        @pl.when(t < last)
        def _():
            to_r.wait_send()
            to_d_right.wait_send()

    to_out_f.wait()
    own_out_f.wait()
    for k in range(2):

        @pl.when(jnp.logical_and(t < last, c == k))
        def _():
            to_right[k].wait_send()

    @pl.when(c == 0)
    def _():
        to_out_c[0].wait_send()
        to_out_c[1].wait_send()
        to_root.wait_send()
        to_next.wait_send()
        to_d_partner.wait_send()

        @pl.when(jnp.logical_or(t == 0, jnp.logical_and(jnp.logical_not(even), t < last)))
        def _():
            to_hub(lb, p).wait_send()

    @pl.when(central)
    def _():
        def drain(q, carry):
            to_owner(q).wait_send()
            return carry

        def drain_two(q, carry):
            to_odd(q).wait_send()
            return carry

        lax.fori_loop(max(1, pairs - 5), pairs, drain, 0)
        lax.fori_loop(direct_from, pairs - 1, drain_two, 0)


def solution(mesh):
    n_t = mesh.shape["tm"]
    fine_set = factors(step_size)
    coarse_set = factors(FACTOR * step_size)
    f32 = jnp.float32

    def vmem(*shape):
        return pltpu.VMEM(shape, f32)

    def on_device(states, start, control, kappa):
        tile = (8, 128)
        return pl.pallas_call(
            functools.partial(kernel, n_t, fine_set, coarse_set),
            out_shape=jax.ShapeDtypeStruct((8, HALF, COLS), f32),
            in_specs=[pl.BlockSpec(memory_space=pl.ANY)] * 4,
            out_specs=pl.BlockSpec(memory_space=pl.ANY),
            scratch_shapes=[
                vmem(7, ROWS, COLS),
                vmem(4, 4, ROWS, 128),
                pltpu.VMEM((COLS, COLS), jnp.bfloat16),
                pltpu.VMEM((COLS, COLS), jnp.bfloat16),
                vmem(*GRID),
                vmem(8, 7, *tile), vmem(9, 6, *tile), vmem(8, 6, *tile),
                vmem(8, 7, *tile), vmem(9, 6, *tile), vmem(4, 8, 6, *tile),
                vmem(8, 7, *tile), vmem(9, 6, *tile), vmem(4, 8, 6, *tile),
                vmem(5, 8, 6, *tile),
                vmem(8, 8, *tile),
                vmem(2, 8, 8, *tile),
                vmem(*GRID),
                vmem(8, *GRID),
                vmem(*GRID), vmem(*GRID), vmem(*GRID),
                vmem(3, *GRID),
                vmem(*GRID), vmem(*GRID),
                vmem(n_t // 2 + 1, *GRID),
                vmem(n_t // 2, *GRID),
                vmem(3, ROWS, COLS),
                vmem(2, ROWS, COLS),
                pltpu.SemaphoreType.DMA((17,)),
                pltpu.SemaphoreType.DMA((17,)),
                pltpu.SemaphoreType.DMA((4,)),
                pltpu.SemaphoreType.DMA((n_t,)),
                pltpu.SemaphoreType.DMA((n_t,)),
                pltpu.SemaphoreType.DMA((n_t,)),
                pltpu.SemaphoreType.REGULAR,
                pltpu.SemaphoreType.REGULAR,
            ],
            compiler_params=pltpu.CompilerParams(
                collective_id=0, has_side_effects=True, vmem_limit_bytes=62 * 2**20
            ),
        )(states, start, control, kappa)

    return jax.shard_map(
        on_device,
        mesh=mesh,
        in_specs=(P("tm", "space", None), P("space", None), P("tm", "space", None), P("space", None)),
        out_specs=P("tm", "space", None),
        check_vma=False,
    )
```

```python
import functools

import jax
import jax.numpy as jnp
import numpy as np
from jax import lax
from jax.experimental import pallas as pl
from jax.experimental.pallas import tpu as pltpu
from jax.sharding import PartitionSpec as P

MESH = pl.DeviceIdType.MESH
CHEB = 6
FACTOR = 4
step_size = 0.1
kappa_top = 1.25
ROWS = 64
COLS = 512
HALF = ROWS // 2
WINDOW = 9
DIRECT = 4
GRID = (8, 4, 8, 128)


def cheb_weights(step_scale):
    highest = 1.0 + 8.0 * step_scale * kappa_top
    centre_value = 0.5 * (highest + 1.0)
    half_width = 0.5 * (highest - 1.0)
    spread_ratio = centre_value / half_width
    rho_prev = 1.0 / spread_ratio
    weights = [(0.0, 1.0 / centre_value)]
    for _ in range(1, CHEB):
        rho_next = 1.0 / (2.0 * spread_ratio - rho_prev)
        weights.append((rho_next * rho_prev, 2.0 * rho_next / half_width))
        rho_prev = rho_next
    return weights


def factors(s):
    poly = np.polynomial.Polynomial
    x, d, one, m = poly([0.0]), poly([0.0]), poly([1.0]), poly([0.0, 1.0])
    for keep, new in cheb_weights(s):
        d = keep * d + new * (one - m * x)
        x = x + d
    lead = x.coef[5]
    roots = x.roots()
    real = [r.real for r in roots if abs(r.imag) < 1e-9]
    pairs = sorted((r.real, r.imag) for r in roots if r.imag > 1e-9)
    assert lead < 0 and len(real) == 1 and len(pairs) == 2
    kap = (-lead * s**6) ** (1.0 / 6.0)
    shifts = [0.0, kap * (1.0 - real[0]) / s] + [kap * (1.0 - p[0]) / s for p in pairs]
    betas = [(kap * p[1] / s) ** 2 for p in pairs]
    return float(kap), [float(v) for v in shifts], [float(v) for v in betas]


def sroll(x, by):
    return pltpu.roll(x, by % 8, 0)


def lroll(x, by):
    return pltpu.roll(x, by % 128, 1)


def put(buf, i, v, val):
    buf[i, v + 2] = val
    if v >= 2:
        buf[i, v - 2] = lroll(val, 1)
    else:
        buf[i, v + 6] = lroll(val, -1)


def pair(src, coefs, at, beta, source, emit):
    d_one, other, left, right, d_two, up_two, low_two, left_two, right_two = coefs
    held, mid = {}, {}

    def y(i, c):
        if (i, c) not in held:
            if i == -1:
                held[i, c] = sroll(y(7, c), 1)
            elif i == 8:
                held[i, c] = sroll(y(0, c), -1)
            else:
                held[i, c] = src[i, c + 2]
        return held[i, c]

    def w(i, c):
        if (i, c) not in mid:
            mid[i, c] = sroll(mid[7, c], 1) if i == -1 else sroll(mid[0, c], -1)
        return mid[i, c]

    first, second = set(), set()
    for i in range(8):
        near, far = (i + 1, i - 1) if i < 7 else (6, 8)
        for c in range(-1, 5):
            k = c + 1
            val = (d_one[at, i, k] * y(i, c) + y(near, c)) + other[i, k] * y(far, c)
            val = val + (left[i, k] * y(i, c - 1) + right[i, k] * y(i, c + 1))
            if source is not None:
                val = val + source(i, c)
            mid[i, c] = val
        first.add(i)
        for j in range(8):
            if j not in second and {(j - 1) % 8, j, (j + 1) % 8} <= first:
                for v in (0, 3, 1, 2):
                    val = (d_two[at, j, v] * w(j, v) + up_two[j, v] * w(j - 1, v)) + low_two[j, v] * w(j + 1, v)
                    val = val + (left_two[j, v] * w(j, v - 1) + right_two[j, v] * w(j, v + 1))
                    if beta is not None:
                        val = val + beta * src[j, v + 2]
                    emit(j, v, val)
                second.add(j)


def solve(buf, tmp, coefs, betas, source, emit):
    pair(buf, coefs, 0, None, source, functools.partial(put, tmp.at[0]))
    pair(tmp.at[0], coefs, 1, betas[0], None, functools.partial(put, tmp.at[1]))
    pair(tmp.at[1], coefs, 2, betas[1], None, emit)


def move_columns(x, table):
    high = x.astype(jnp.bfloat16)
    rest = x - high.astype(jnp.float32)
    middle = rest.astype(jnp.bfloat16)
    low = (rest - middle.astype(jnp.float32)).astype(jnp.bfloat16)
    stacked = jnp.concatenate([high, middle, low], 0)
    out = jnp.dot(stacked, table, preferred_element_type=jnp.float32)
    n = x.shape[0]
    return (out[:n] + out[n : 2 * n]) + out[2 * n :]


def kernel(
    n_t, fine_set, coarse_set,
    states, start, control, kappa, out,
    nat, xp, table_in, table_out, kp, fx0, fy0, c0, share, fine_coefs, coarse,
    g, ub, tmp, old, wd, rb, nb, lb, dp, eb, fb, lbuf, es, nat_f, nat_c,
    ss, rs, ls, lrecv, esend, esend_two, credit, go,
):
    t = lax.axis_index("tm")
    c = lax.axis_index("space")
    last = n_t - 1
    central = jnp.logical_and(t == last, c == 0)
    pairs = n_t // 2
    p = t // 2
    even = t % 2 == 0
    raw_slot, pair_slot = pairs - 1, pairs
    partner = (t, 1 - c)
    right = (t + 1, 0 * c)
    hub = (0 * t + last, 0 * c)
    mine = pl.multiple_of(c * HALF, HALF)
    theirs = pl.multiple_of((1 - c) * HALF, HALF)

    def remote(src, dst, k, dev):
        return pltpu.make_async_remote_copy(
            src_ref=src, dst_ref=dst, send_sem=ss.at[k], recv_sem=rs.at[k], device_id=dev, device_id_type=MESH
        )

    barrier = pltpu.get_barrier_semaphore()
    pl.semaphore_signal(barrier, inc=1, device_id=partner, device_id_type=MESH)

    @pl.when(jnp.logical_and(c == 0, t > 0))
    def _():
        pl.semaphore_signal(barrier, inc=1, device_id=(t - 1, 0 * c), device_id_type=MESH)
        pl.semaphore_signal(barrier, inc=1, device_id=(t - 1, 0 * c + 1), device_id_type=MESH)

    @pl.when(jnp.logical_and(c == 0, t < last))
    def _():
        pl.semaphore_signal(barrier, inc=1, device_id=hub, device_id_type=MESH)

    def local(src, dst, k):
        return pltpu.make_async_copy(src, dst, ls.at[k])

    own_control = local(control.at[pl.ds(4 * c, 4)], nat.at[pl.ds(0, 4), pl.ds(mine, HALF), :], 0)
    own_kappa = local(kappa, nat.at[6, pl.ds(mine, HALF), :], 1)
    own_first = local(states.at[3], nat.at[5, pl.ds(mine, HALF), :], 2)
    own_start = local(start, nat.at[4, pl.ds(mine, HALF), :], 3)
    own_root = local(states.at[3], nat.at[4, pl.ds(mine, HALF), :], 2)
    own_next = local(states.at[7], nat.at[5, pl.ds(mine, HALF), :], 3)
    own_kappa.start()
    own_control.start()

    @pl.when(c == 0)
    def _():
        own_first.start()

        @pl.when(t == 0)
        def _():
            own_start.start()

    @pl.when(c == 1)
    def _():
        own_root.start()
        own_next.start()

    down = lax.broadcasted_iota(jnp.int32, (COLS, COLS), 0)
    across = lax.broadcasted_iota(jnp.int32, (COLS, COLS), 1)
    table_in[...] = jnp.where(down == 4 * (across % 128) + across // 128, 1.0, 0.0).astype(jnp.bfloat16)
    table_out[...] = jnp.where(across == 4 * (down % 128) + down // 128, 1.0, 0.0).astype(jnp.bfloat16)

    pl.semaphore_wait(barrier, 1 + jnp.where(t < last, 1, 0) + jnp.where(central, last, 0))

    to_control = remote(control.at[pl.ds(4 * (1 - c), 4)], nat.at[pl.ds(0, 4), pl.ds(mine, HALF), :], 0, partner)
    to_kappa = remote(kappa, nat.at[6, pl.ds(mine, HALF), :], 3, partner)
    to_root = remote(states.at[3], nat.at[4, pl.ds(mine, HALF), :], 1, partner)
    to_next = remote(states.at[7], nat.at[5, pl.ds(mine, HALF), :], 2, partner)
    to_first = remote(states.at[3], nat.at[5, pl.ds(mine, HALF), :], 2, partner)
    to_start = remote(start, nat.at[4, pl.ds(mine, HALF), :], 1, partner)
    to_right = [remote(states.at[7], nat.at[4, pl.ds(k * HALF, HALF), :], 5 + k, right) for k in range(2)]

    for k in range(2):

        @pl.when(jnp.logical_and(t < last, c == k))
        def _():
            to_right[k].start()

    to_kappa.start()

    @pl.when(c == 0)
    def _():
        to_root.start()
        to_next.start()

    @pl.when(c == 1)
    def _():
        to_first.start()

        @pl.when(t == 0)
        def _():
            to_start.start()

    to_control.start()

    @pl.when(central)
    def _():
        def give(k, carry):
            pl.semaphore_signal(credit, inc=1, device_id=(k, 0 * c), device_id_type=MESH)
            return carry

        give(0, 0)
        lax.fori_loop(0, min(WINDOW, pairs - 1), lambda k, carry: give(2 * k + 1, carry), 0)

    def to_layout(x, at, use):
        moved = move_columns(x, table_in[...])
        for v in range(4):
            xp[at, v] = moved[:, 128 * v : 128 * (v + 1)]
        for i in range(8):
            for v in range(4):
                use(i, v, xp[at, v, pl.ds(i, 8, stride=8), :])

    def from_layout(at, give):
        for i in range(8):
            for v in range(4):
                xp[at, v, pl.ds(i, 8, stride=8), :] = give(i, v)
        return move_columns(jnp.concatenate([xp[at, v] for v in range(4)], 1), table_out[...])

    own_kappa.wait()
    to_kappa.wait()

    def hold_kappa(i, v, val):
        kp[i, v] = val

    to_layout(nat[6], 0, hold_kappa)
    lane = lax.broadcasted_iota(jnp.int32, (8, 128), 1)
    sub = lax.broadcasted_iota(jnp.int32, (8, 128), 0)
    zero = jnp.zeros((8, 128), jnp.float32)
    for i in range(8):
        row = [kp[i, v] for v in range(4)]
        after = jnp.where(lane < 127, lroll(row[0], -1), zero)
        before = jnp.where(lane > 0, lroll(row[3], 1), zero)
        wide = [before] + row + [after]
        side = [0.5 * (wide[k] + wide[k + 1]) for k in range(5)]
        inner_right = jnp.where(lane < 127, side[4], zero)
        inner = [jnp.where(lane > 0, side[0], zero), side[1], side[2], side[3], inner_right]
        for k in range(5):
            fx0[i, k + 1] = inner[k]
        fx0[i, 0] = lroll(side[3], 1)
        fx0[i, 6] = lroll(side[1], -1)
        for v in range(4):
            if i == 0:
                above = jnp.where(sub > 0, sroll(kp[7, v], 1), zero)
            else:
                above = kp[i - 1, v]
            if i == 7:
                below = jnp.where(sub < 7, sroll(kp[0, v], -1), zero)
            else:
                below = kp[i + 1, v]
            up = 0.5 * (above + row[v])
            low = 0.5 * (row[v] + below)
            centre = ((up + low) + side[v]) + side[v + 1]
            pieces = [(c0, i, centre), (fy0, i, jnp.where(sub > 0, up, zero) if i == 0 else up)]
            if i == 7:
                pieces.append((fy0, 8, jnp.where(sub < 7, low, zero)))
            for ref, at, val in pieces:
                ref[at, v + 1] = val
                if v == 3:
                    ref[at, 0] = lroll(val, 1)
                if v == 0:
                    ref[at, 5] = lroll(val, -1)

    def fill(kap, shifts, coefs):
        d_one, other, left, right, d_two, up_two, low_two, left_two, right_two = coefs

        def fx(i, k):
            return fx0[i, k] * (-kap)

        def fy(i, k):
            return fy0[i, k] * (-kap)

        def held_by(i, k):
            if i == -1:
                return sroll(fy(7, k), 1)
            if i == 8:
                return sroll(fy(1, k), -1)
            return fy(i + 1, k) if i < 7 else fy(7, k)

        for i in range(8):
            for k in range(6):
                inverse = 1.0 / held_by(i, k)
                share[i, k] = inverse
                for n, at in enumerate((0, 2, 3)):
                    d_one[n, i, k] = (c0[i, k] * kap + shifts[at]) * inverse
                other[i, k] = fy(i if i < 7 else 8, k) * inverse
                left[i, k] = fx(i, k) * inverse
                right[i, k] = fx(i, k + 1) * inverse
            for v in range(4):
                k = v + 1
                for n, at in enumerate((1, 2, 3)):
                    d_two[n, i, v] = (c0[i, k] * kap + shifts[at]) * held_by(i, k)
                up_two[i, v] = fy(i, k) * held_by(i - 1, k)
                low_two[i, v] = fy(i + 1, k) * held_by(i + 1, k)
                left_two[i, v] = fx(i, k) * held_by(i, k - 1)
                right_two[i, v] = fx(i, k + 1) * held_by(i, k + 1)

    fill(coarse_set[0], coarse_set[1], coarse)
    fill(fine_set[0], fine_set[1], fine_coefs)

    @pl.when(c == 0)
    def _():
        own_first.wait()
        to_first.wait_recv()

        @pl.when(t == 0)
        def _():
            own_start.wait()
            to_start.wait_recv()

        @pl.when(t > 0)
        def _():
            to_right[0].wait_recv()
            to_right[1].wait_recv()

    @pl.when(c == 1)
    def _():
        own_root.wait()
        own_next.wait()
        to_root.wait_recv()
        to_next.wait_recv()

    to_layout(nat[4], 0, functools.partial(put, ub))

    def hold_old(i, v, val):
        old[i, v] = val

    to_layout(nat[5], 1, hold_old)
    own_control.wait()
    to_control.wait()

    def hold_source(j, i, v, val):
        val = val * (-fine_set[0])
        g[j, i, v + 1] = val * share[i, v + 1]
        if v == 3:
            g[j, i, 0] = lroll(val, 1) * share[i, 0]
        if v == 0:
            g[j, i, 5] = lroll(val, -1) * share[i, 5]

    for j in range(4):
        to_layout(nat[j], j, functools.partial(hold_source, j))
    g[4] = jnp.zeros(g.shape[1:], jnp.float32)

    def fine(j, carry):
        @pl.when(j == 4)
        def _():
            for i in range(8):
                for v in range(4):
                    put(ub, i, v, wd[3, i, v] - old[i, v])

        source = g.at[jnp.minimum(j, 4)]

        def emit(i, v, val):
            val = val + ub[i, v + 2]
            put(ub, i, v, val)
            wd[j, i, v] = val

        solve(ub, tmp, fine_coefs, fine_set[2], lambda i, k: source[i, k + 1], emit)
        return carry

    lax.fori_loop(0, 8, fine, 0)

    to_r = remote(wd.at[7], rb, 7, partner)
    to_c = remote(wd.at[3], nb, 8, partner)
    to_d_partner = remote(wd.at[pl.ds(4, 3)], dp, 9, partner)
    to_d_right = remote(wd.at[pl.ds(4, 3)], dp, 9, right)

    def to_hub(src, slot):
        return pltpu.make_async_remote_copy(
            src_ref=src, dst_ref=lbuf.at[slot], send_sem=ss.at[13], recv_sem=lrecv.at[slot],
            device_id=hub, device_id_type=MESH,
        )

    to_second = pltpu.make_async_remote_copy(
        src_ref=lb, dst_ref=lbuf.at[pair_slot], send_sem=ss.at[15], recv_sem=lrecv.at[pair_slot],
        device_id=right, device_id_type=MESH,
    )

    @pl.when(c == 1)
    def _():
        @pl.when(t < last)
        def _():
            to_r.start()

        to_c.start()

        @pl.when(t < last)
        def _():
            pl.semaphore_wait(go, 1)
            to_d_right.start()


    def coarse_solve(emit):
        solve(ub, tmp, coarse, coarse_set[2], None, emit)

    def load(ref):
        for i in range(8):
            for v in range(4):
                put(ub, i, v, ref[i, v])

    def advance(n):
        def one(k, carry):
            coarse_solve(lambda i, v, val: put(ub, i, v, val + ub[i, v + 2]))
            return carry

        lax.fori_loop(0, n, one, 0)

    def add(dst, other):
        for i in range(8):
            for v in range(4):
                dst[i, v] = ub[i, v + 2] + other[i, v]

    @pl.when(jnp.logical_and(c == 0, t < last))
    def _():
        advance(1)
        to_r.wait_recv()
        add(lb, rb)

        @pl.when(even)
        def _():
            to_second.start()

            @pl.when(t == 0)
            def _():
                pl.semaphore_wait(credit, 1)
                to_hub(lb, raw_slot).start()

            to_second.wait_send()

        @pl.when(jnp.logical_not(even))
        def _():
            @pl.when(t > 1)
            def _():
                to_second.wait_recv()
                load(lbuf.at[pair_slot])
                advance(2)
                add(lb, lb)

            @pl.when(t == 1)
            def _():
                pl.semaphore_wait(credit, 1)
                to_hub(lb, p).start()
                to_hub(lb, p).wait_send()

        pl.semaphore_signal(go, inc=1, device_id=partner, device_id_type=MESH)

        @pl.when(jnp.logical_and(jnp.logical_not(even), t > 1))
        def _():
            pl.semaphore_wait(credit, 1)
            to_hub(lb, p).start()

    @pl.when(c == 0)
    def _():
        to_d_partner.start()

    to_out_f = remote(
        nat_f.at[:, pl.ds(theirs, HALF), :], out.at[pl.ds(4 * c, 3)], 10, partner
    )

    own_out_f = local(nat_f.at[:, pl.ds(mine, HALF), :], out.at[pl.ds(4 * c, 3)], 0)

    def f_points():
        has = jnp.logical_or(c == 1, t > 0)

        @pl.when(has)
        def _():
            to_d_partner.wait_recv()

        @pl.when(jnp.logical_not(has))
        def _():
            dp[...] = jnp.zeros(dp.shape, jnp.float32)

        for j in range(3):
            nat_f[j] = from_layout(j, lambda i, v: wd[j, i, v] + dp[j, i, v])
        to_out_f.start()
        own_out_f.start()

    @pl.when(jnp.logical_not(central))
    def _():
        f_points()

    def to_owner(q):
        return pltpu.make_async_remote_copy(
            src_ref=es.at[q], dst_ref=eb, send_sem=esend.at[q], recv_sem=rs.at[14],
            device_id=(2 * q, 0 * c), device_id_type=MESH,
        )

    def to_odd(q):
        return pltpu.make_async_remote_copy(
            src_ref=es.at[q], dst_ref=eb, send_sem=esend_two.at[q], recv_sem=rs.at[14],
            device_id=(2 * q + 1, 0 * c), device_id_type=MESH,
        )

    forward = pltpu.make_async_remote_copy(
        src_ref=eb, dst_ref=eb, send_sem=ss.at[16], recv_sem=rs.at[14], device_id=right, device_id_type=MESH
    )
    direct_from = max(1, pairs - DIRECT)

    @pl.when(central)
    def _():
        to_hub(lb, raw_slot).wait_recv()
        load(lbuf.at[raw_slot])

        def turns(n, added, kept):
            for k in range(n):
                if k < n - 1:
                    coarse_solve(lambda i, v, val: put(ub, i, v, val + ub[i, v + 2]))
                else:

                    def emit(i, v, val):
                        val = val + (ub[i, v + 2] + added[i, v])
                        put(ub, i, v, val)
                        kept[i, v] = val

                    coarse_solve(emit)

        def send(q):
            to_owner(q).start()

            @pl.when(jnp.logical_and(q >= direct_from, q < pairs - 1))
            def _():
                to_odd(q).start()

        to_hub(lb, 0).wait_recv()
        turns(2, lbuf.at[0], es.at[1])

        def turn(q, carry):
            send(q)

            @pl.when(q + WINDOW - 1 < pairs - 1)
            def _():
                pl.semaphore_signal(credit, inc=1, device_id=(2 * (q + WINDOW) - 1, 0 * c), device_id_type=MESH)

            @pl.when(q == min(5, pairs - 2))
            def _():
                f_points()

            @pl.when(q >= 5)
            def _():
                to_owner(q - 4).wait_send()

            to_hub(lb, q).wait_recv()
            turns(4, lbuf.at[q], es.at[q + 1])
            return carry

        lax.fori_loop(1, pairs - 1, turn, 0)
        send(pairs - 1)
        to_second.wait_recv()
        turns(2, lbuf.at[pair_slot], eb)

    to_out_c = [
        remote(nat_c.at[k, pl.ds(HALF, HALF), :], out.at[4 * k + 3], 11 + k, partner) for k in range(2)
    ]
    own_out_c = [local(nat_c.at[k, pl.ds(0, HALF), :], out.at[4 * k + 3], 1 + k) for k in range(2)]

    @pl.when(c == 0)
    def _():
        to_c.wait_recv()

        @pl.when(t == 0)
        def _():
            eb[...] = jnp.zeros(eb.shape, jnp.float32)

        @pl.when(t == 1)
        def _():
            to_second.wait_recv()
            eb[...] = lbuf[pair_slot]

        @pl.when(jnp.logical_and(t > 1, t < last))
        def _():
            to_owner(0).wait_recv()

        @pl.when(jnp.logical_and(even, jnp.logical_and(p > 0, p < direct_from)))
        def _():
            forward.start()

        @pl.when(t < last)
        def _():
            load(eb)

        @pl.when(jnp.logical_and(jnp.logical_not(even), jnp.logical_and(t > 1, t < last)))
        def _():
            advance(2)
            add(eb, lbuf.at[pair_slot])
            load(eb)

        nat_c[0] = from_layout(0, lambda i, v: wd[3, i, v] + eb[i, v])

        def emit(i, v, val):
            fb[i, v] = (val + ub[i, v + 2]) + wd[7, i, v]

        coarse_solve(emit)
        nat_c[1] = from_layout(1, lambda i, v: nb[i, v] + fb[i, v])
        for k in range(2):
            to_out_c[k].start()
            own_out_c[k].start()
        own_out_c[0].wait()
        own_out_c[1].wait()

        @pl.when(jnp.logical_and(even, jnp.logical_and(p > 0, p < direct_from)))
        def _():
            forward.wait_send()

    @pl.when(c == 1)
    def _():
        to_out_c[0].wait_recv()
        to_out_c[1].wait_recv()
        to_c.wait_send()
        to_first.wait_send()

        @pl.when(t == 0)
        def _():
            to_start.wait_send()

        @pl.when(t < last)
        def _():
            to_r.wait_send()
            to_d_right.wait_send()

    to_out_f.wait()
    own_out_f.wait()
    for k in range(2):

        @pl.when(jnp.logical_and(t < last, c == k))
        def _():
            to_right[k].wait_send()

    @pl.when(c == 0)
    def _():
        to_out_c[0].wait_send()
        to_out_c[1].wait_send()
        to_root.wait_send()
        to_next.wait_send()
        to_d_partner.wait_send()

        @pl.when(jnp.logical_or(t == 0, jnp.logical_and(jnp.logical_not(even), jnp.logical_and(t > 1, t < last))))
        def _():
            to_hub(lb, p).wait_send()

    @pl.when(central)
    def _():
        def drain(q, carry):
            to_owner(q).wait_send()
            return carry

        def drain_two(q, carry):
            to_odd(q).wait_send()
            return carry

        lax.fori_loop(max(1, pairs - 5), pairs, drain, 0)
        lax.fori_loop(direct_from, pairs - 1, drain_two, 0)


def solution(mesh):
    n_t = mesh.shape["tm"]
    fine_set = factors(step_size)
    coarse_set = factors(FACTOR * step_size)
    f32 = jnp.float32

    def vmem(*shape):
        return pltpu.VMEM(shape, f32)

    def on_device(states, start, control, kappa):
        tile = (8, 128)

        def coefs():
            one = [vmem(3, 8, 6, *tile)] + [vmem(8, 6, *tile)] * 3
            return one + [vmem(3, 8, 4, *tile)] + [vmem(8, 4, *tile)] * 4

        return pl.pallas_call(
            functools.partial(kernel, n_t, fine_set, coarse_set),
            out_shape=jax.ShapeDtypeStruct((8, HALF, COLS), f32),
            in_specs=[pl.BlockSpec(memory_space=pl.ANY)] * 4,
            out_specs=pl.BlockSpec(memory_space=pl.ANY),
            scratch_shapes=[
                vmem(7, ROWS, COLS),
                vmem(4, 4, ROWS, 128),
                pltpu.VMEM((COLS, COLS), jnp.bfloat16),
                pltpu.VMEM((COLS, COLS), jnp.bfloat16),
                vmem(*GRID),
                vmem(8, 7, *tile), vmem(9, 6, *tile), vmem(8, 6, *tile),
                vmem(8, 6, *tile),
                coefs(),
                coefs(),
                vmem(5, 8, 6, *tile),
                vmem(8, 8, *tile),
                vmem(2, 8, 8, *tile),
                vmem(*GRID),
                vmem(8, *GRID),
                vmem(*GRID), vmem(*GRID), vmem(*GRID),
                vmem(3, *GRID),
                vmem(*GRID), vmem(*GRID),
                vmem(n_t // 2 + 1, *GRID),
                vmem(n_t // 2, *GRID),
                vmem(3, ROWS, COLS),
                vmem(2, ROWS, COLS),
                pltpu.SemaphoreType.DMA((17,)),
                pltpu.SemaphoreType.DMA((17,)),
                pltpu.SemaphoreType.DMA((4,)),
                pltpu.SemaphoreType.DMA((n_t,)),
                pltpu.SemaphoreType.DMA((n_t,)),
                pltpu.SemaphoreType.DMA((n_t,)),
                pltpu.SemaphoreType.REGULAR,
                pltpu.SemaphoreType.REGULAR,
            ],
            compiler_params=pltpu.CompilerParams(
                collective_id=0, has_side_effects=True, vmem_limit_bytes=62 * 2**20
            ),
        )(states, start, control, kappa)

    return jax.shard_map(
        on_device,
        mesh=mesh,
        in_specs=(P("tm", "space", None), P("space", None), P("tm", "space", None), P("space", None)),
        out_specs=P("tm", "space", None),
        check_vma=False,
    )
```

```python
import functools

import jax
import jax.numpy as jnp
import numpy as np
from jax import lax
from jax.experimental import pallas as pl
from jax.experimental.pallas import tpu as pltpu
from jax.sharding import PartitionSpec as P

MESH = pl.DeviceIdType.MESH
CHEB = 6
FACTOR = 4
step_size = 0.1
kappa_top = 1.25
ROWS = 64
COLS = 512
HALF = ROWS // 2
WINDOW = 9
DIRECT = 4
GRID = (8, 4, 8, 128)


def cheb_weights(step_scale):
    highest = 1.0 + 8.0 * step_scale * kappa_top
    centre_value = 0.5 * (highest + 1.0)
    half_width = 0.5 * (highest - 1.0)
    spread_ratio = centre_value / half_width
    rho_prev = 1.0 / spread_ratio
    weights = [(0.0, 1.0 / centre_value)]
    for _ in range(1, CHEB):
        rho_next = 1.0 / (2.0 * spread_ratio - rho_prev)
        weights.append((rho_next * rho_prev, 2.0 * rho_next / half_width))
        rho_prev = rho_next
    return weights


def factors(s):
    poly = np.polynomial.Polynomial
    x, d, one, m = poly([0.0]), poly([0.0]), poly([1.0]), poly([0.0, 1.0])
    for keep, new in cheb_weights(s):
        d = keep * d + new * (one - m * x)
        x = x + d
    lead = x.coef[5]
    roots = x.roots()
    real = [r.real for r in roots if abs(r.imag) < 1e-9]
    pairs = sorted((r.real, r.imag) for r in roots if r.imag > 1e-9)
    assert lead < 0 and len(real) == 1 and len(pairs) == 2
    kap = (-lead * s**6) ** (1.0 / 6.0)
    shifts = [0.0, kap * (1.0 - real[0]) / s] + [kap * (1.0 - p[0]) / s for p in pairs]
    betas = [(kap * p[1] / s) ** 2 for p in pairs]
    return float(kap), [float(v) for v in shifts], [float(v) for v in betas]


def sroll(x, by):
    return pltpu.roll(x, by % 8, 0)


def lroll(x, by):
    return pltpu.roll(x, by % 128, 1)


def put(buf, i, v, val):
    buf[i, v + 2] = val
    if v >= 2:
        buf[i, v - 2] = lroll(val, 1)
    else:
        buf[i, v + 6] = lroll(val, -1)


def pair(src, coefs, at, beta, source, emit):
    d_one, other, left, right, d_two, up_two, low_two, left_two, right_two = coefs
    held, mid = {}, {}

    def y(i, c):
        if (i, c) not in held:
            if i == -1:
                held[i, c] = sroll(y(7, c), 1)
            elif i == 8:
                held[i, c] = sroll(y(0, c), -1)
            else:
                held[i, c] = src[i, c + 2]
        return held[i, c]

    def w(i, c):
        if (i, c) not in mid:
            mid[i, c] = sroll(mid[7, c], 1) if i == -1 else sroll(mid[0, c], -1)
        return mid[i, c]

    first, second = set(), set()
    for i in range(8):
        near, far = (i + 1, i - 1) if i < 7 else (6, 8)
        for c in range(-1, 5):
            k = c + 1
            val = (d_one[at, i, k] * y(i, c) + y(near, c)) + other[i, k] * y(far, c)
            val = val + (left[i, k] * y(i, c - 1) + right[i, k] * y(i, c + 1))
            if source is not None:
                val = val + source(i, c)
            mid[i, c] = val
        first.add(i)
        for j in range(8):
            if j not in second and {(j - 1) % 8, j, (j + 1) % 8} <= first:
                for v in (0, 3, 1, 2):
                    val = (d_two[at, j, v] * w(j, v) + up_two[j, v] * w(j - 1, v)) + low_two[j, v] * w(j + 1, v)
                    val = val + (left_two[j, v] * w(j, v - 1) + right_two[j, v] * w(j, v + 1))
                    if beta is not None:
                        val = val + beta * src[j, v + 2]
                    emit(j, v, val)
                second.add(j)


def solve(buf, tmp, coefs, betas, source, emit):
    pair(buf, coefs, 0, None, source, functools.partial(put, tmp.at[0]))
    pair(tmp.at[0], coefs, 1, betas[0], None, functools.partial(put, tmp.at[1]))
    pair(tmp.at[1], coefs, 2, betas[1], None, emit)


def move_columns(x, table):
    high = x.astype(jnp.bfloat16)
    rest = x - high.astype(jnp.float32)
    middle = rest.astype(jnp.bfloat16)
    low = (rest - middle.astype(jnp.float32)).astype(jnp.bfloat16)
    stacked = jnp.concatenate([high, middle, low], 0)
    out = jnp.dot(stacked, table, preferred_element_type=jnp.float32)
    n = x.shape[0]
    return (out[:n] + out[n : 2 * n]) + out[2 * n :]


def kernel(
    n_t, fine_set, coarse_set,
    states, start, control, kappa, out,
    nat, xp, table_in, table_out, kp, fx0, fy0, c0, share, fine_coefs, coarse,
    g, ub, tmp, old, wd, rb, nb, lb, dp, eb, fb, lbuf, es, nat_f, nat_c,
    ss, rs, ls, lrecv, esend, esend_two, credit, go,
):
    t = lax.axis_index("tm")
    c = lax.axis_index("space")
    last = n_t - 1
    central = jnp.logical_and(t == last, c == 0)
    pairs = n_t // 2
    p = t // 2
    even = t % 2 == 0
    raw_slot, pair_slot = pairs - 1, pairs
    partner = (t, 1 - c)
    right = (t + 1, 0 * c)
    hub = (0 * t + last, 0 * c)
    mine = pl.multiple_of(c * HALF, HALF)
    theirs = pl.multiple_of((1 - c) * HALF, HALF)

    def remote(src, dst, k, dev):
        return pltpu.make_async_remote_copy(
            src_ref=src, dst_ref=dst, send_sem=ss.at[k], recv_sem=rs.at[k], device_id=dev, device_id_type=MESH
        )

    barrier = pltpu.get_barrier_semaphore()
    pl.semaphore_signal(barrier, inc=1, device_id=partner, device_id_type=MESH)

    @pl.when(jnp.logical_and(c == 0, t > 0))
    def _():
        pl.semaphore_signal(barrier, inc=1, device_id=(t - 1, 0 * c), device_id_type=MESH)
        pl.semaphore_signal(barrier, inc=1, device_id=(t - 1, 0 * c + 1), device_id_type=MESH)

    @pl.when(jnp.logical_and(c == 0, t < last))
    def _():
        pl.semaphore_signal(barrier, inc=1, device_id=hub, device_id_type=MESH)

    def local(src, dst, k):
        return pltpu.make_async_copy(src, dst, ls.at[k])

    own_control = local(control.at[pl.ds(4 * c, 4)], nat.at[pl.ds(0, 4), pl.ds(mine, HALF), :], 0)
    own_kappa = local(kappa, nat.at[6, pl.ds(mine, HALF), :], 1)
    own_first = local(states.at[3], nat.at[5, pl.ds(mine, HALF), :], 2)
    own_start = local(start, nat.at[4, pl.ds(mine, HALF), :], 3)
    own_root = local(states.at[3], nat.at[4, pl.ds(mine, HALF), :], 2)
    own_next = local(states.at[7], nat.at[5, pl.ds(mine, HALF), :], 3)
    own_kappa.start()
    own_control.start()

    @pl.when(c == 0)
    def _():
        own_first.start()

        @pl.when(t == 0)
        def _():
            own_start.start()

    @pl.when(c == 1)
    def _():
        own_root.start()
        own_next.start()

    down = lax.broadcasted_iota(jnp.int32, (COLS, COLS), 0)
    across = lax.broadcasted_iota(jnp.int32, (COLS, COLS), 1)
    table_in[...] = jnp.where(down == 4 * (across % 128) + across // 128, 1.0, 0.0).astype(jnp.bfloat16)
    table_out[...] = jnp.where(across == 4 * (down % 128) + down // 128, 1.0, 0.0).astype(jnp.bfloat16)

    pl.semaphore_wait(barrier, 1 + jnp.where(t < last, 1, 0) + jnp.where(central, last, 0))

    to_control = remote(control.at[pl.ds(4 * (1 - c), 4)], nat.at[pl.ds(0, 4), pl.ds(mine, HALF), :], 0, partner)
    to_kappa = remote(kappa, nat.at[6, pl.ds(mine, HALF), :], 3, partner)
    to_root = remote(states.at[3], nat.at[4, pl.ds(mine, HALF), :], 1, partner)
    to_next = remote(states.at[7], nat.at[5, pl.ds(mine, HALF), :], 2, partner)
    to_first = remote(states.at[3], nat.at[5, pl.ds(mine, HALF), :], 2, partner)
    to_start = remote(start, nat.at[4, pl.ds(mine, HALF), :], 1, partner)
    to_right = [remote(states.at[7], nat.at[4, pl.ds(k * HALF, HALF), :], 5 + k, right) for k in range(2)]

    for k in range(2):

        @pl.when(jnp.logical_and(t < last, c == k))
        def _():
            to_right[k].start()

    to_kappa.start()

    @pl.when(c == 0)
    def _():
        to_root.start()
        to_next.start()

    @pl.when(c == 1)
    def _():
        to_first.start()

        @pl.when(t == 0)
        def _():
            to_start.start()

    to_control.start()

    @pl.when(central)
    def _():
        def give(k, carry):
            pl.semaphore_signal(credit, inc=1, device_id=(k, 0 * c), device_id_type=MESH)
            return carry

        give(0, 0)
        lax.fori_loop(0, min(WINDOW, pairs - 1), lambda k, carry: give(2 * k + 1, carry), 0)

    def to_layout(x, at, use):
        moved = move_columns(x, table_in[...])
        for v in range(4):
            xp[at, v] = moved[:, 128 * v : 128 * (v + 1)]
        for i in range(8):
            for v in range(4):
                use(i, v, xp[at, v, pl.ds(i, 8, stride=8), :])

    def from_layout(at, give):
        for i in range(8):
            for v in range(4):
                xp[at, v, pl.ds(i, 8, stride=8), :] = give(i, v)
        return move_columns(jnp.concatenate([xp[at, v] for v in range(4)], 1), table_out[...])

    own_kappa.wait()
    to_kappa.wait()

    def hold_kappa(i, v, val):
        kp[i, v] = val

    to_layout(nat[6], 0, hold_kappa)
    lane = lax.broadcasted_iota(jnp.int32, (8, 128), 1)
    sub = lax.broadcasted_iota(jnp.int32, (8, 128), 0)
    zero = jnp.zeros((8, 128), jnp.float32)
    for i in range(8):
        row = [kp[i, v] for v in range(4)]
        after = jnp.where(lane < 127, lroll(row[0], -1), zero)
        before = jnp.where(lane > 0, lroll(row[3], 1), zero)
        wide = [before] + row + [after]
        side = [0.5 * (wide[k] + wide[k + 1]) for k in range(5)]
        inner_right = jnp.where(lane < 127, side[4], zero)
        inner = [jnp.where(lane > 0, side[0], zero), side[1], side[2], side[3], inner_right]
        for k in range(5):
            fx0[i, k + 1] = inner[k]
        fx0[i, 0] = lroll(side[3], 1)
        fx0[i, 6] = lroll(side[1], -1)
        for v in range(4):
            if i == 0:
                above = jnp.where(sub > 0, sroll(kp[7, v], 1), zero)
            else:
                above = kp[i - 1, v]
            if i == 7:
                below = jnp.where(sub < 7, sroll(kp[0, v], -1), zero)
            else:
                below = kp[i + 1, v]
            up = 0.5 * (above + row[v])
            low = 0.5 * (row[v] + below)
            centre = ((up + low) + side[v]) + side[v + 1]
            pieces = [(c0, i, centre), (fy0, i, jnp.where(sub > 0, up, zero) if i == 0 else up)]
            if i == 7:
                pieces.append((fy0, 8, jnp.where(sub < 7, low, zero)))
            for ref, at, val in pieces:
                ref[at, v + 1] = val
                if v == 3:
                    ref[at, 0] = lroll(val, 1)
                if v == 0:
                    ref[at, 5] = lroll(val, -1)

    def fill(kap, shifts, coefs):
        d_one, other, left, right, d_two, up_two, low_two, left_two, right_two = coefs

        def fx(i, k):
            return fx0[i, k] * (-kap)

        def fy(i, k):
            return fy0[i, k] * (-kap)

        def held_by(i, k):
            if i == -1:
                return sroll(fy(7, k), 1)
            if i == 8:
                return sroll(fy(1, k), -1)
            return fy(i + 1, k) if i < 7 else fy(7, k)

        for i in range(8):
            for k in range(6):
                inverse = 1.0 / held_by(i, k)
                share[i, k] = inverse
                for n, at in enumerate((0, 2, 3)):
                    d_one[n, i, k] = (c0[i, k] * kap + shifts[at]) * inverse
                other[i, k] = fy(i if i < 7 else 8, k) * inverse
                left[i, k] = fx(i, k) * inverse
                right[i, k] = fx(i, k + 1) * inverse
            for v in range(4):
                k = v + 1
                for n, at in enumerate((1, 2, 3)):
                    d_two[n, i, v] = (c0[i, k] * kap + shifts[at]) * held_by(i, k)
                up_two[i, v] = fy(i, k) * held_by(i - 1, k)
                low_two[i, v] = fy(i + 1, k) * held_by(i + 1, k)
                left_two[i, v] = fx(i, k) * held_by(i, k - 1)
                right_two[i, v] = fx(i, k + 1) * held_by(i, k + 1)

    fill(coarse_set[0], coarse_set[1], coarse)
    fill(fine_set[0], fine_set[1], fine_coefs)

    @pl.when(c == 0)
    def _():
        own_first.wait()
        to_first.wait_recv()

        @pl.when(t == 0)
        def _():
            own_start.wait()
            to_start.wait_recv()

        @pl.when(t > 0)
        def _():
            to_right[0].wait_recv()
            to_right[1].wait_recv()

    @pl.when(c == 1)
    def _():
        own_root.wait()
        own_next.wait()
        to_root.wait_recv()
        to_next.wait_recv()

    to_layout(nat[4], 0, functools.partial(put, ub))

    def hold_old(i, v, val):
        old[i, v] = val

    to_layout(nat[5], 1, hold_old)
    own_control.wait()
    to_control.wait()

    def hold_source(j, i, v, val):
        val = val * (-fine_set[0])
        g[j, i, v + 1] = val * share[i, v + 1]
        if v == 3:
            g[j, i, 0] = lroll(val, 1) * share[i, 0]
        if v == 0:
            g[j, i, 5] = lroll(val, -1) * share[i, 5]

    for j in range(4):
        to_layout(nat[j], j, functools.partial(hold_source, j))
    g[4] = jnp.zeros(g.shape[1:], jnp.float32)

    def fine(j, carry):
        @pl.when(j == 4)
        def _():
            for i in range(8):
                for v in range(4):
                    put(ub, i, v, wd[3, i, v] - old[i, v])

        source = g.at[jnp.minimum(j, 4)]

        def emit(i, v, val):
            val = val + ub[i, v + 2]
            put(ub, i, v, val)
            wd[j, i, v] = val

        solve(ub, tmp, fine_coefs, fine_set[2], lambda i, k: source[i, k + 1], emit)
        return carry

    lax.fori_loop(0, 8, fine, 0)

    to_r = remote(wd.at[7], rb, 7, partner)
    to_c = remote(wd.at[3], nb, 8, partner)
    to_d_partner = remote(wd.at[pl.ds(4, 3)], dp, 9, partner)
    to_d_right = remote(wd.at[pl.ds(4, 3)], dp, 9, right)

    def to_hub(src, slot):
        return pltpu.make_async_remote_copy(
            src_ref=src, dst_ref=lbuf.at[slot], send_sem=ss.at[13], recv_sem=lrecv.at[slot],
            device_id=hub, device_id_type=MESH,
        )

    to_second = pltpu.make_async_remote_copy(
        src_ref=lb, dst_ref=lbuf.at[pair_slot], send_sem=ss.at[15], recv_sem=lrecv.at[pair_slot],
        device_id=right, device_id_type=MESH,
    )

    @pl.when(c == 1)
    def _():
        @pl.when(t < last)
        def _():
            to_r.start()

        to_c.start()

        @pl.when(t < last)
        def _():
            pl.semaphore_wait(go, 1)
            to_d_right.start()


    def coarse_solve(emit):
        solve(ub, tmp, coarse, coarse_set[2], None, emit)

    def load(ref):
        for i in range(8):
            for v in range(4):
                put(ub, i, v, ref[i, v])

    def advance(n):
        def one(k, carry):
            coarse_solve(lambda i, v, val: put(ub, i, v, val + ub[i, v + 2]))
            return carry

        lax.fori_loop(0, n, one, 0)

    def add(dst, other):
        for i in range(8):
            for v in range(4):
                dst[i, v] = ub[i, v + 2] + other[i, v]

    @pl.when(jnp.logical_and(c == 0, t < last))
    def _():
        advance(1)
        to_r.wait_recv()
        add(lb, rb)

        @pl.when(even)
        def _():
            to_second.start()

            @pl.when(t == 0)
            def _():
                pl.semaphore_wait(credit, 1)
                to_hub(lb, raw_slot).start()

            to_second.wait_send()

        @pl.when(jnp.logical_not(even))
        def _():
            @pl.when(t > 1)
            def _():
                to_second.wait_recv()
                load(lbuf.at[pair_slot])
                advance(2)
                add(lb, lb)

            @pl.when(t == 1)
            def _():
                pl.semaphore_wait(credit, 1)
                to_hub(lb, p).start()
                to_hub(lb, p).wait_send()

        pl.semaphore_signal(go, inc=1, device_id=partner, device_id_type=MESH)

        @pl.when(jnp.logical_and(jnp.logical_not(even), t > 1))
        def _():
            pl.semaphore_wait(credit, 1)
            to_hub(lb, p).start()

    @pl.when(c == 0)
    def _():
        to_d_partner.start()

    to_out_f = remote(
        nat_f.at[:, pl.ds(theirs, HALF), :], out.at[pl.ds(4 * c, 3)], 10, partner
    )

    own_out_f = local(nat_f.at[:, pl.ds(mine, HALF), :], out.at[pl.ds(4 * c, 3)], 0)

    def f_points():
        has = jnp.logical_or(c == 1, t > 0)

        @pl.when(has)
        def _():
            to_d_partner.wait_recv()

        @pl.when(jnp.logical_not(has))
        def _():
            dp[...] = jnp.zeros(dp.shape, jnp.float32)

        for j in range(3):
            nat_f[j] = from_layout(j, lambda i, v: wd[j, i, v] + dp[j, i, v])
        to_out_f.start()
        own_out_f.start()

    @pl.when(jnp.logical_not(central))
    def _():
        f_points()

    def to_owner(q):
        return pltpu.make_async_remote_copy(
            src_ref=es.at[q], dst_ref=eb, send_sem=esend.at[q], recv_sem=rs.at[14],
            device_id=(2 * q, 0 * c), device_id_type=MESH,
        )

    def to_odd(q):
        return pltpu.make_async_remote_copy(
            src_ref=es.at[q], dst_ref=eb, send_sem=esend_two.at[q], recv_sem=rs.at[14],
            device_id=(2 * q + 1, 0 * c), device_id_type=MESH,
        )

    forward = pltpu.make_async_remote_copy(
        src_ref=eb, dst_ref=eb, send_sem=ss.at[16], recv_sem=rs.at[14], device_id=right, device_id_type=MESH
    )
    direct_from = max(1, pairs - DIRECT)

    @pl.when(central)
    def _():
        to_hub(lb, raw_slot).wait_recv()
        load(lbuf.at[raw_slot])

        def turns(n, added, kept):
            for k in range(n):
                if k < n - 1:
                    coarse_solve(lambda i, v, val: put(ub, i, v, val + ub[i, v + 2]))
                else:

                    def emit(i, v, val):
                        val = val + (ub[i, v + 2] + added[i, v])
                        put(ub, i, v, val)
                        kept[i, v] = val

                    coarse_solve(emit)

        def send(q):
            to_owner(q).start()

            @pl.when(jnp.logical_and(q >= direct_from, q < pairs - 1))
            def _():
                to_odd(q).start()

        to_hub(lb, 0).wait_recv()
        turns(2, lbuf.at[0], es.at[1])

        def turn(q, carry):
            send(q)

            @pl.when(q + WINDOW - 1 < pairs - 1)
            def _():
                pl.semaphore_signal(credit, inc=1, device_id=(2 * (q + WINDOW) - 1, 0 * c), device_id_type=MESH)

            @pl.when(q >= 5)
            def _():
                to_owner(q - 4).wait_send()

            to_hub(lb, q).wait_recv()
            turns(4, lbuf.at[q], es.at[q + 1])
            return carry

        lax.fori_loop(1, pairs - 1, turn, 0)
        send(pairs - 1)
        to_second.wait_recv()
        turns(2, lbuf.at[pair_slot], eb)

    to_out_c = [
        remote(nat_c.at[k, pl.ds(HALF, HALF), :], out.at[4 * k + 3], 11 + k, partner) for k in range(2)
    ]
    own_out_c = [local(nat_c.at[k, pl.ds(0, HALF), :], out.at[4 * k + 3], 1 + k) for k in range(2)]

    @pl.when(c == 0)
    def _():
        to_c.wait_recv()

        @pl.when(t == 0)
        def _():
            eb[...] = jnp.zeros(eb.shape, jnp.float32)

        @pl.when(t == 1)
        def _():
            to_second.wait_recv()
            eb[...] = lbuf[pair_slot]

        @pl.when(jnp.logical_and(t > 1, t < last))
        def _():
            to_owner(0).wait_recv()

        @pl.when(jnp.logical_and(even, jnp.logical_and(p > 0, p < direct_from)))
        def _():
            forward.start()

        @pl.when(t < last)
        def _():
            load(eb)

        @pl.when(jnp.logical_and(jnp.logical_not(even), jnp.logical_and(t > 1, t < last)))
        def _():
            advance(2)
            add(eb, lbuf.at[pair_slot])
            load(eb)

        nat_c[0] = from_layout(0, lambda i, v: wd[3, i, v] + eb[i, v])

        def emit(i, v, val):
            fb[i, v] = (val + ub[i, v + 2]) + wd[7, i, v]

        coarse_solve(emit)
        nat_c[1] = from_layout(1, lambda i, v: nb[i, v] + fb[i, v])
        for k in range(2):
            to_out_c[k].start()
            own_out_c[k].start()
        own_out_c[0].wait()
        own_out_c[1].wait()

        @pl.when(jnp.logical_and(even, jnp.logical_and(p > 0, p < direct_from)))
        def _():
            forward.wait_send()

    @pl.when(central)
    def _():
        f_points()

    @pl.when(c == 1)
    def _():
        to_out_c[0].wait_recv()
        to_out_c[1].wait_recv()
        to_c.wait_send()
        to_first.wait_send()

        @pl.when(t == 0)
        def _():
            to_start.wait_send()

        @pl.when(t < last)
        def _():
            to_r.wait_send()
            to_d_right.wait_send()

    to_out_f.wait()
    own_out_f.wait()
    for k in range(2):

        @pl.when(jnp.logical_and(t < last, c == k))
        def _():
            to_right[k].wait_send()

    @pl.when(c == 0)
    def _():
        to_out_c[0].wait_send()
        to_out_c[1].wait_send()
        to_root.wait_send()
        to_next.wait_send()
        to_d_partner.wait_send()

        @pl.when(jnp.logical_or(t == 0, jnp.logical_and(jnp.logical_not(even), jnp.logical_and(t > 1, t < last))))
        def _():
            to_hub(lb, p).wait_send()

    @pl.when(central)
    def _():
        def drain(q, carry):
            to_owner(q).wait_send()
            return carry

        def drain_two(q, carry):
            to_odd(q).wait_send()
            return carry

        lax.fori_loop(max(1, pairs - 5), pairs, drain, 0)
        lax.fori_loop(direct_from, pairs - 1, drain_two, 0)


def solution(mesh):
    n_t = mesh.shape["tm"]
    fine_set = factors(step_size)
    coarse_set = factors(FACTOR * step_size)
    f32 = jnp.float32

    def vmem(*shape):
        return pltpu.VMEM(shape, f32)

    def on_device(states, start, control, kappa):
        tile = (8, 128)

        def coefs():
            one = [vmem(3, 8, 6, *tile)] + [vmem(8, 6, *tile)] * 3
            return one + [vmem(3, 8, 4, *tile)] + [vmem(8, 4, *tile)] * 4

        return pl.pallas_call(
            functools.partial(kernel, n_t, fine_set, coarse_set),
            out_shape=jax.ShapeDtypeStruct((8, HALF, COLS), f32),
            in_specs=[pl.BlockSpec(memory_space=pl.ANY)] * 4,
            out_specs=pl.BlockSpec(memory_space=pl.ANY),
            scratch_shapes=[
                vmem(7, ROWS, COLS),
                vmem(4, 4, ROWS, 128),
                pltpu.VMEM((COLS, COLS), jnp.bfloat16),
                pltpu.VMEM((COLS, COLS), jnp.bfloat16),
                vmem(*GRID),
                vmem(8, 7, *tile), vmem(9, 6, *tile), vmem(8, 6, *tile),
                vmem(8, 6, *tile),
                coefs(),
                coefs(),
                vmem(5, 8, 6, *tile),
                vmem(8, 8, *tile),
                vmem(2, 8, 8, *tile),
                vmem(*GRID),
                vmem(8, *GRID),
                vmem(*GRID), vmem(*GRID), vmem(*GRID),
                vmem(3, *GRID),
                vmem(*GRID), vmem(*GRID),
                vmem(n_t // 2 + 1, *GRID),
                vmem(n_t // 2, *GRID),
                vmem(3, ROWS, COLS),
                vmem(2, ROWS, COLS),
                pltpu.SemaphoreType.DMA((17,)),
                pltpu.SemaphoreType.DMA((17,)),
                pltpu.SemaphoreType.DMA((4,)),
                pltpu.SemaphoreType.DMA((n_t,)),
                pltpu.SemaphoreType.DMA((n_t,)),
                pltpu.SemaphoreType.DMA((n_t,)),
                pltpu.SemaphoreType.REGULAR,
                pltpu.SemaphoreType.REGULAR,
            ],
            compiler_params=pltpu.CompilerParams(
                collective_id=0, has_side_effects=True, vmem_limit_bytes=62 * 2**20
            ),
        )(states, start, control, kappa)

    return jax.shard_map(
        on_device,
        mesh=mesh,
        in_specs=(P("tm", "space", None), P("space", None), P("tm", "space", None), P("space", None)),
        out_specs=P("tm", "space", None),
        check_vma=False,
    )
```
